256 devices in a mesh: gz: 32 (over z_lo, y, x), gy: 8 (over z_hi, core).
Axes of the slice: x: 4, y: 4, z: 8 (z_hi: 4, z_lo: 2; z = z_hi * 2 + z_lo), core: 2. Of those that a mesh axis runs over, the one named last changes fastest.
Arguments:
- fodf: float32 [192, 64, 64, 128], P(None, 'gy', 'gz'), may hold values from 0 to 21, as said below
- directions: float32 [3, 192], replicated, may hold values from -1 to 1, as said below
- signs: int32 [3, 192], replicated, may hold values from -1 to 1, as said below
Outputs:
- enhanced: float32 [192, 64, 64, 128], P(None, 'gy', 'gz')
The draws below stay inside these ranges and needn't reach their ends.
Inputs may be any that keep to these rules, and one draw needn't show every extreme that they name: `fodf`: Non-negative densities. `directions`: unit vectors; orientation k + 96 is the antipode of orientation k; no component is zero. `signs`: each sign is the sign of the matching component of directions; along each axis exactly 96 orientations have sign 1.
All inputs are finite; a program needn't handle non-finite values.
Results may differ from the reference program's by a relative error of at most 0.0003.
Values sent between devices are 32-bit elements; how exact they have to be, the bound alone decides.
A program may use at most 64 MiB of HBM per device.

```python
import math
import jax
import jax.numpy as jnp
from jax import lax

K = 192
LMAX = 8
X = 128
ITERS = 4
NY = 64
NZ = 64


def orientation_pairs(key):
    halves = K // 2
    signs_half = 2 * jax.random.randint(jax.random.fold_in(key, 17), (3, halves), 0, 2) - 1
    magnitude = jax.random.uniform(jax.random.fold_in(key, 29), (3, halves), jnp.float32, 0.15, 1.0)
    vectors = signs_half.astype(jnp.float32) * magnitude
    vectors = vectors / jnp.sqrt(jnp.sum(vectors * vectors, axis=0, keepdims=True))
    return (jnp.concatenate([vectors, -vectors], 1), jnp.concatenate([signs_half, -signs_half], 1).astype(jnp.int32))


def draw_directions(key, part):
    return orientation_pairs(key)[0]


def draw_signs(key, part):
    return orientation_pairs(key)[1]


def draw_fodf(key, part):
    grid_shape = (K, NY, NZ, X)
    normal_part = jnp.clip(jax.random.normal(jax.random.fold_in(key, 5), grid_shape, jnp.float32), -5.0, 5.0)
    return jnp.exp(0.6 * normal_part)


def setup_inputs(seed: int = 0) -> dict:
    key_list = jax.random.split(jax.random.key(seed), 4)
    return {
        "fodf": draw_fodf(jax.random.fold_in(key_list[3], 71), 0),
        "directions": draw_directions(jax.random.fold_in(key_list[3], 71), 0),
        "signs": draw_signs(jax.random.fold_in(key_list[3], 71), 0),
    }


TIME_STEP = 0.5
DIFFUSION = 0.02

def double_factorial(value):
    result = 1
    while value > 1:
        result = result * value
        value = value - 2
    return result

def harmonic_rows(directions):
    along_x, along_y, along_z = (directions[0], directions[1], directions[2])
    cosines = [jnp.ones_like(along_x)]
    sines = [jnp.zeros_like(along_x)]
    for order in range(1, LMAX + 1):
        cosines.append(cosines[-1] * along_x - sines[-1] * along_y)
        sines.append(cosines[-2] * along_y + sines[-1] * along_x)
    legendre = {}
    for order in range(LMAX + 1):
        legendre[order, order] = double_factorial(2 * order - 1) * jnp.ones_like(along_z)
        if order + 1 <= LMAX:
            legendre[order + 1, order] = (2 * order + 1) * along_z * legendre[order, order]
        for degree in range(order + 2, LMAX + 1):
            legendre[degree, order] = ((2 * degree - 1) * along_z * legendre[degree - 1, order] - (degree + order - 1) * legendre[degree - 2, order]) / (degree - order)
    basis_rows = []
    eigen_values = []
    for degree in range(0, LMAX + 1, 2):
        for order in range(degree + 1):
            weight_norm = math.sqrt((2 * degree + 1) * math.factorial(degree - order) / math.factorial(degree + order))
            basis_rows.append(weight_norm * legendre[degree, order] * cosines[order])
            eigen_values.append(-float(degree * (degree + 1)))
            if order > 0:
                basis_rows.append(weight_norm * legendre[degree, order] * sines[order])
                eigen_values.append(-float(degree * (degree + 1)))
    return (jnp.stack(basis_rows, 0), jnp.array(eigen_values, dtype=directions.dtype))

def angular_maps(directions):
    basis, eigen_values = harmonic_rows(directions)
    gram = jnp.dot(basis, basis.T, precision=lax.Precision.HIGHEST)
    chol_lower = jnp.linalg.cholesky(gram)
    partial_solve = lax.linalg.triangular_solve(chol_lower, basis, left_side=True, lower=True)
    analysis = lax.linalg.triangular_solve(chol_lower, partial_solve, left_side=True, lower=True, transpose_a=True)
    synthesis = basis.T * eigen_values[None, :]
    return (analysis, synthesis)

def reference(fodf, directions, signs):
    analysis, synthesis = angular_maps(directions)
    speeds = jnp.abs(directions).T
    upwinds = signs.T
    field = fodf
    for sweep in range(ITERS):
        coeffs = jnp.dot(analysis, field.reshape(K, -1), precision=lax.Precision.HIGHEST)

        def single(items):
            row, speed_row, upwind_row, synth_row = items
            padded = jnp.pad(row, 1)
            center = row
            pairs = [(padded[1:-1, 1:-1, :-2], padded[1:-1, 1:-1, 2:]), (padded[:-2, 1:-1, 1:-1], padded[2:, 1:-1, 1:-1]), (padded[1:-1, :-2, 1:-1], padded[1:-1, 2:, 1:-1])]
            transport = jnp.zeros_like(center)
            for axis_number in range(3):
                beneath, beyond = pairs[axis_number]
                chosen = jnp.where(upwind_row[axis_number] > 0, beneath, beyond)
                transport = transport + speed_row[axis_number] * (center - chosen)
            angular = jnp.dot(synth_row, coeffs, precision=lax.Precision.HIGHEST).reshape(row.shape)
            return center - TIME_STEP * transport + TIME_STEP * DIFFUSION * angular
        field = lax.map(single, (field, speeds, upwinds, synthesis))
    return field
```

```python
import math

import jax
import jax.numpy as jnp
from jax import lax
from jax.experimental import pallas as pl
from jax.experimental.pallas import tpu as pltpu
from jax.sharding import PartitionSpec as P

LMAX = 8
ITERS = 4
TIME_STEP = 0.5
DIFFUSION = 0.02

HALF = 96
LANES = 128
MODES = 45
MODES_PAD = 48
CHUNK = 16
HIGHEST = lax.Precision.HIGHEST
MESH = pl.DeviceIdType.MESH

AX, AY, AZ, CENTER, SX, SY, SZ = range(7)


def double_factorial(value):
    result = 1
    while value > 1:
        result = result * value
        value = value - 2
    return result


def harmonic_rows(along_x, along_y, along_z):
    cosines = [jnp.ones_like(along_x)]
    sines = [jnp.zeros_like(along_x)]
    for order in range(1, LMAX + 1):
        cosines.append(cosines[-1] * along_x - sines[-1] * along_y)
        sines.append(cosines[-2] * along_y + sines[-1] * along_x)
    legendre = {}
    for order in range(LMAX + 1):
        legendre[order, order] = double_factorial(2 * order - 1) * jnp.ones_like(along_z)
        if order + 1 <= LMAX:
            legendre[order + 1, order] = (2 * order + 1) * along_z * legendre[order, order]
        for degree in range(order + 2, LMAX + 1):
            legendre[degree, order] = (
                (2 * degree - 1) * along_z * legendre[degree - 1, order]
                - (degree + order - 1) * legendre[degree - 2, order]
            ) * (1.0 / (degree - order))
    rows = []
    for degree in range(0, LMAX + 1, 2):
        for order in range(degree + 1):
            norm = math.sqrt(
                (2 * degree + 1) * math.factorial(degree - order) / math.factorial(degree + order)
            )
            eigenvalue = -float(degree * (degree + 1))
            scaled = norm * legendre[degree, order]
            rows.append((scaled * cosines[order], eigenvalue))
            if order > 0:
                rows.append((scaled * sines[order], eigenvalue))
    return rows


def angular_matrix(dirs, basis, scaled, left, right):
    valid = lax.broadcasted_iota(jnp.int32, (1, LANES), 1) < HALF
    basis[...] = jnp.zeros_like(basis)
    scaled[...] = jnp.zeros_like(scaled)
    left[...] = jnp.zeros_like(left)
    right[...] = jnp.zeros_like(right)
    along = [dirs[a : a + 1, 0:LANES] for a in range(3)]
    for j, (row, eigenvalue) in enumerate(harmonic_rows(*along)):
        row = jnp.where(valid, row, 0.0)
        basis[j : j + 1, :] = row
        scaled[j : j + 1, :] = (TIME_STEP * DIFFUSION * eigenvalue) * row
    b, s = basis[...], scaled[...]
    gram = 2.0 * lax.dot_general(
        b, jnp.concatenate([b, jnp.zeros((LANES - MODES_PAD, LANES), jnp.float32)], 0),
        (((1,), (1,)), ((), ())), precision=HIGHEST, preferred_element_type=jnp.float32,
    )
    index = lax.broadcasted_iota(jnp.int32, (MODES_PAD, LANES), 0)
    for k in range(MODES):
        column = jnp.broadcast_to(gram[:, k : k + 1], (MODES_PAD, LANES))
        inverse = 1.0 / column[k : k + 1, :]
        gram_row, b_row, s_row = gram[k : k + 1, :], b[k : k + 1, :], s[k : k + 1, :]
        left[k : k + 1, :] = s_row
        right[k : k + 1, :] = b_row * inverse
        if k + 1 < MODES:
            factor = jnp.where(index > k, column, 0.0)
            gram = gram - factor * (gram_row * inverse)
            b = b - factor * (b_row * inverse)
            s = s - factor * (s_row * inverse)
    return lax.dot_general(
        left[...].T, right[...], (((1,), (0,)), ((), ())), precision=HIGHEST,
        preferred_element_type=jnp.float32,
    )


def kernel(
    fodf, dirs_hbm, signs_hbm, out,
    stage, dirs, signs, coef, basis, scaled, left, right, mat_hi, mat_lo, angular, p, q, u, v,
    in_sem, small_sem, z_send, z_recv, y_send, y_recv,
):
    ny, nz = p.shape[2], u.shape[1]
    gz, gy = lax.axis_index("gz"), lax.axis_index("gy")
    gz_last, gy_last = lax.axis_size("gz") - 1, lax.axis_size("gy") - 1
    below, above = gz > 0, gz < gz_last
    before, after = gy > 0, gy < gy_last

    def load(r):
        return pltpu.make_async_copy(fodf.at[:, r, 0, :], stage.at[r], in_sem.at[r])

    def store(r):
        return pltpu.make_async_copy(stage.at[r], out.at[:, r, 0, :], in_sem.at[r])

    def z_up(s, y):
        return pltpu.make_async_remote_copy(
            p.at[s, nz, y], p.at[s, 0, y], z_send.at[0, s, y], z_recv.at[0, s, y],
            device_id=(gz + 1, gy), device_id_type=MESH,
        )

    def z_down(s, y):
        return pltpu.make_async_remote_copy(
            q.at[s, 0, y], q.at[s, nz, y], z_send.at[1, s, y], z_recv.at[1, s, y],
            device_id=(gz - 1, gy), device_id_type=MESH,
        )

    def y_up(s):
        return pltpu.make_async_remote_copy(
            u.at[s, :, ny], u.at[s, :, 0], y_send.at[0, s], y_recv.at[0, s],
            device_id=(gz, gy + 1), device_id_type=MESH,
        )

    def y_down(s):
        return pltpu.make_async_remote_copy(
            v.at[s, :, 0], v.at[s, :, ny], y_send.at[1, s], y_recv.at[1, s],
            device_id=(gz, gy - 1), device_id_type=MESH,
        )

    def send(s, y):
        pl.when(above)(lambda: z_up(s, y).start())
        pl.when(below)(lambda: z_down(s, y).start())
        pl.when(jnp.logical_and(y == 0, before))(lambda: y_down(s).start())
        pl.when(jnp.logical_and(y == ny - 1, after))(lambda: y_up(s).start())

    def receive(s, y):
        pl.when(below)(lambda: z_up(s, y).wait_recv())
        pl.when(above)(lambda: z_down(s, y).wait_recv())
        pl.when(jnp.logical_and(y == 0, before))(lambda: y_up(s).wait_recv())
        pl.when(jnp.logical_and(y == ny - 1, after))(lambda: y_down(s).wait_recv())

    small = [
        pltpu.make_async_copy(dirs_hbm, dirs, small_sem.at[0]),
        pltpu.make_async_copy(signs_hbm, signs, small_sem.at[1]),
    ]
    for copy in small:
        copy.start()
    for r in range(ny * nz):
        load(r).start()

    barrier = pltpu.get_barrier_semaphore()
    for there, target in (
        (below, (gz - 1, gy)), (above, (gz + 1, gy)), (before, (gz, gy - 1)), (after, (gz, gy + 1)),
    ):
        @pl.when(there)
        def _():
            pl.semaphore_signal(barrier, inc=1, device_id=target, device_id_type=MESH)

    @pl.when(gz == 0)
    def _():
        p[:, 0] = jnp.zeros_like(p[:, 0])

    @pl.when(gz == gz_last)
    def _():
        q[:, nz] = jnp.zeros_like(q[:, nz])

    @pl.when(gy == 0)
    def _():
        u[:, :, 0] = jnp.zeros_like(u[:, :, 0])

    @pl.when(gy == gy_last)
    def _():
        v[:, :, ny] = jnp.zeros_like(v[:, :, ny])

    for copy in small:
        copy.wait()
    half_speed = TIME_STEP * jnp.abs(dirs[:, 0:LANES])
    sign = signs[:, 0:LANES].astype(jnp.float32)
    sign_z = sign[2:3]
    rows = [half_speed[0:1], half_speed[1:2], half_speed[2:3]]
    rows.append(1.0 - (rows[0] + rows[1] + rows[2]))
    rows += [sign[0:1] * sign_z, sign[1:2] * sign_z, sign_z]
    table = jnp.concatenate(rows + [jnp.zeros((LANES - len(rows), LANES), jnp.float32)], 0).T
    for c in range(len(rows)):
        coef[c] = jnp.broadcast_to(table[0:HALF, c : c + 1], (HALF, LANES))

    peers = sum(there.astype(jnp.int32) for there in (below, above, before, after))
    pl.semaphore_wait(barrier, peers)

    def first(y, carry):
        for z in range(nz):
            r = y * nz + z
            load(r).wait()
            for c in range(0, HALF, CHUNK):
                lines = slice(c, c + CHUNK)
                one, other = stage[r, c : c + CHUNK, :], stage[r, HALF + c : HALF + c + CHUNK, :]
                upward, along_y = coef[SZ, lines] > 0, coef[SY, lines] > 0
                up, down = jnp.where(upward, one, other), jnp.where(upward, other, one)
                p[0, z + 1, y, lines] = up
                q[0, z, y, lines] = down
                u[0, z, y + 1, lines] = jnp.where(along_y, up, down)
                v[0, z, y, lines] = jnp.where(along_y, down, up)
        send(0, y)
        return carry

    lax.fori_loop(0, ny, first, 0)

    matrix = angular_matrix(dirs, basis, scaled, left, right)[0:HALF, 0:HALF]
    high = matrix.astype(jnp.bfloat16)
    mat_hi[...] = high
    mat_lo[...] = (matrix - high.astype(jnp.float32)).astype(jnp.bfloat16)

    lane = lax.broadcasted_iota(jnp.int32, (CHUNK, LANES), 1)

    def advance(s, y, last):
        total = jnp.concatenate([p[s, z + 1, y] + q[s, z, y] for z in range(nz)], 1)
        total_hi = total.astype(jnp.bfloat16)
        total_lo = (total - total_hi.astype(jnp.float32)).astype(jnp.bfloat16)
        hi, lo = mat_hi[...], mat_lo[...]
        angular[...] = (
            jnp.dot(hi, total_hi, preferred_element_type=jnp.float32)
            + jnp.dot(hi, total_lo, preferred_element_type=jnp.float32)
            + jnp.dot(lo, total_hi, preferred_element_type=jnp.float32)
        )
        receive(s, y)
        for z in range(nz):
            for c in range(0, HALF, CHUNK):
                lines = slice(c, c + CHUNK)
                up, down = p[s, z + 1, y, lines], q[s, z, y, lines]
                along_x, along_y = coef[SX, lines] > 0, coef[SY, lines] > 0
                rising, falling = jnp.where(along_x, up, down), jnp.where(along_x, down, up)
                rising = jnp.where(lane == 0, 0.0, pltpu.roll(rising, 1, 1))
                falling = jnp.where(lane == LANES - 1, 0.0, pltpu.roll(falling, LANES - 1, 1))
                y_low, y_high = u[s, z, y, lines], v[s, z, y + 1, lines]
                ang = angular[lines, z * LANES : (z + 1) * LANES]
                ax, ay, az, center = (coef[i, lines] for i in (AX, AY, AZ, CENTER))
                new_up = (
                    center * up + ang + ax * jnp.where(along_x, rising, falling)
                    + ay * jnp.where(along_y, y_low, y_high) + az * p[s, z, y, lines]
                )
                new_down = (
                    center * down + ang + ax * jnp.where(along_x, falling, rising)
                    + ay * jnp.where(along_y, y_high, y_low) + az * q[s, z + 1, y, lines]
                )
                if last:
                    r = y * nz + z
                    upward = coef[SZ, lines] > 0
                    stage[r, c : c + CHUNK, :] = jnp.where(upward, new_up, new_down)
                    stage[r, HALF + c : HALF + c + CHUNK, :] = jnp.where(upward, new_down, new_up)
                else:
                    p[s + 1, z + 1, y, lines] = new_up
                    q[s + 1, z, y, lines] = new_down
                    u[s + 1, z, y + 1, lines] = jnp.where(along_y, new_up, new_down)
                    v[s + 1, z, y, lines] = jnp.where(along_y, new_down, new_up)

    def middle(i, carry):
        s, y = i // ny, i % ny
        advance(s, y, False)
        send(s + 1, y)
        return carry

    lax.fori_loop(0, (ITERS - 1) * ny, middle, 0)

    def final(y, carry):
        advance(ITERS - 1, y, True)
        for z in range(nz):
            store(y * nz + z).start()
        return carry

    lax.fori_loop(0, ny, final, 0)

    def sent(i, carry):
        s, y = i // ny, i % ny
        pl.when(above)(lambda: z_up(s, y).wait_send())
        pl.when(below)(lambda: z_down(s, y).wait_send())
        return carry

    lax.fori_loop(0, ITERS * ny, sent, 0)
    for s in range(ITERS):
        pl.when(after)(lambda: y_up(s).wait_send())
        pl.when(before)(lambda: y_down(s).wait_send())
    for r in range(ny * nz):
        store(r).wait()


def shards(fodf, directions, signs):
    orientations, ny, nz, _ = fodf.shape
    f32, vmem, dma = jnp.float32, pltpu.VMEM, pltpu.SemaphoreType.DMA
    rows = fodf.reshape(orientations, ny * nz, 1, LANES)
    enhanced = pl.pallas_call(
        kernel,
        out_shape=jax.ShapeDtypeStruct(rows.shape, f32),
        in_specs=[pl.BlockSpec(memory_space=pl.ANY)] * 3,
        out_specs=pl.BlockSpec(memory_space=pl.ANY),
        scratch_shapes=[
            vmem((ny * nz, orientations, LANES), f32),
            vmem((3, orientations), f32),
            vmem((3, orientations), jnp.int32),
            vmem((7, HALF, LANES), f32),
            vmem((MODES_PAD, LANES), f32),
            vmem((MODES_PAD, LANES), f32),
            vmem((MODES_PAD, LANES), f32),
            vmem((MODES_PAD, LANES), f32),
            vmem((HALF, HALF), jnp.bfloat16),
            vmem((HALF, HALF), jnp.bfloat16),
            vmem((HALF, nz * LANES), f32),
            vmem((ITERS, nz + 1, ny, HALF, LANES), f32),
            vmem((ITERS, nz + 1, ny, HALF, LANES), f32),
            vmem((ITERS, nz, ny + 1, HALF, LANES), f32),
            vmem((ITERS, nz, ny + 1, HALF, LANES), f32),
            dma((ny * nz,)),
            dma((2,)),
            dma((2, ITERS, ny)),
            dma((2, ITERS, ny)),
            dma((2, ITERS)),
            dma((2, ITERS)),
        ],
        compiler_params=pltpu.CompilerParams(
            collective_id=0, has_side_effects=True, vmem_limit_bytes=48 * 1024 * 1024
        ),
    )(rows, directions, signs)
    return enhanced.reshape(fodf.shape)


def solution(mesh):
    placed = (P(None, "gy", "gz", None), P(), P())
    return jax.shard_map(
        shards, mesh=mesh, in_specs=placed, out_specs=P(None, "gy", "gz", None), check_vma=False
    )
```

```python
import math

import jax
import jax.numpy as jnp
from jax import lax
from jax.experimental import pallas as pl
from jax.experimental.pallas import tpu as pltpu
from jax.sharding import PartitionSpec as P

LMAX = 8
ITERS = 4
TIME_STEP = 0.5
DIFFUSION = 0.02

HALF = 96
LANES = 128
MODES = 45
MODES_PAD = 48
CHUNK = 16
RELAYED = 3
HIGHEST = lax.Precision.HIGHEST
MESH = pl.DeviceIdType.MESH

AX, AY, AZ, CENTER, SX, SY, SZ = range(7)


def double_factorial(value):
    result = 1
    while value > 1:
        result = result * value
        value = value - 2
    return result


def harmonic_rows(along_x, along_y, along_z):
    cosines = [jnp.ones_like(along_x)]
    sines = [jnp.zeros_like(along_x)]
    for order in range(1, LMAX + 1):
        cosines.append(cosines[-1] * along_x - sines[-1] * along_y)
        sines.append(cosines[-2] * along_y + sines[-1] * along_x)
    legendre = {}
    for order in range(LMAX + 1):
        legendre[order, order] = double_factorial(2 * order - 1) * jnp.ones_like(along_z)
        if order + 1 <= LMAX:
            legendre[order + 1, order] = (2 * order + 1) * along_z * legendre[order, order]
        for degree in range(order + 2, LMAX + 1):
            legendre[degree, order] = (
                (2 * degree - 1) * along_z * legendre[degree - 1, order]
                - (degree + order - 1) * legendre[degree - 2, order]
            ) * (1.0 / (degree - order))
    rows = []
    for degree in range(0, LMAX + 1, 2):
        for order in range(degree + 1):
            norm = math.sqrt(
                (2 * degree + 1) * math.factorial(degree - order) / math.factorial(degree + order)
            )
            eigenvalue = -float(degree * (degree + 1))
            scaled = norm * legendre[degree, order]
            rows.append((scaled * cosines[order], eigenvalue))
            if order > 0:
                rows.append((scaled * sines[order], eigenvalue))
    return rows


def angular_matrix(dirs, basis, scaled, left, right):
    valid = lax.broadcasted_iota(jnp.int32, (1, LANES), 1) < HALF
    basis[...] = jnp.zeros_like(basis)
    scaled[...] = jnp.zeros_like(scaled)
    left[...] = jnp.zeros_like(left)
    right[...] = jnp.zeros_like(right)
    along = [dirs[a : a + 1, 0:LANES] for a in range(3)]
    for j, (row, eigenvalue) in enumerate(harmonic_rows(*along)):
        row = jnp.where(valid, row, 0.0)
        basis[j : j + 1, :] = row
        scaled[j : j + 1, :] = (TIME_STEP * DIFFUSION * eigenvalue) * row
    b, s = basis[...], scaled[...]
    gram = 2.0 * lax.dot_general(
        b, jnp.concatenate([b, jnp.zeros((LANES - MODES_PAD, LANES), jnp.float32)], 0),
        (((1,), (1,)), ((), ())), precision=HIGHEST, preferred_element_type=jnp.float32,
    )
    index = lax.broadcasted_iota(jnp.int32, (MODES_PAD, LANES), 0)
    for k in range(MODES):
        column = jnp.broadcast_to(gram[:, k : k + 1], (MODES_PAD, LANES))
        inverse = 1.0 / column[k : k + 1, :]
        gram_row, b_row, s_row = gram[k : k + 1, :], b[k : k + 1, :], s[k : k + 1, :]
        left[k : k + 1, :] = s_row
        right[k : k + 1, :] = b_row * inverse
        if k + 1 < MODES:
            factor = jnp.where(index > k, column, 0.0)
            gram = gram - factor * (gram_row * inverse)
            b = b - factor * (b_row * inverse)
            s = s - factor * (s_row * inverse)
    return lax.dot_general(
        left[...].T, right[...], (((1,), (0,)), ((), ())), precision=HIGHEST,
        preferred_element_type=jnp.float32,
    )


def kernel(
    fodf, dirs_hbm, signs_hbm, out,
    stage, dirs, signs, coef, basis, scaled, left, right, mat_hi, mat_lo, angular, p, q, u, v, relay,
    in_sem, small_sem, z_send, z_recv, y_send, y_recv, relay_recv,
):
    ny, nz = p.shape[2], u.shape[1]
    kept = ny - RELAYED
    gz, gy = lax.axis_index("gz"), lax.axis_index("gy")
    gz_last, gy_last = lax.axis_size("gz") - 1, lax.axis_size("gy") - 1
    below, above = gz > 0, gz < gz_last
    before, after = gy > 0, gy < gy_last
    seam_high = (gz_last + 1) // 2
    seam_low = seam_high - 1
    is_low, is_high, is_first, is_last = gz == seam_low, gz == seam_high, gz == 0, gz == gz_last

    def load(r):
        return pltpu.make_async_copy(fodf.at[:, r, 0, :], stage.at[r], in_sem.at[r])

    def store(r):
        return pltpu.make_async_copy(stage.at[r], out.at[:, r, 0, :], in_sem.at[r])

    def z_up(s, y):
        return pltpu.make_async_remote_copy(
            p.at[s, nz, y], p.at[s, 0, y], z_send.at[0, s, y], z_recv.at[0, s, y],
            device_id=(gz + 1, gy), device_id_type=MESH,
        )

    def z_down(s, y):
        return pltpu.make_async_remote_copy(
            q.at[s, 0, y], q.at[s, nz, y], z_send.at[1, s, y], z_recv.at[1, s, y],
            device_id=(gz - 1, gy), device_id_type=MESH,
        )

    def relay_up(s, y):
        return pltpu.make_async_remote_copy(
            p.at[s, nz, y], relay.at[s, y - kept], z_send.at[0, s, y], relay_recv.at[s, y - kept],
            device_id=(gz_last, gy), device_id_type=MESH,
        )

    def relay_down(s, y):
        return pltpu.make_async_remote_copy(
            q.at[s, 0, y], relay.at[s, y - kept], z_send.at[1, s, y], relay_recv.at[s, y - kept],
            device_id=(0, gy), device_id_type=MESH,
        )

    def forward_up(s, y):
        return pltpu.make_async_remote_copy(
            relay.at[s, y - kept], p.at[s, 0, y], z_send.at[0, s, y], z_recv.at[0, s, y],
            device_id=(seam_high, gy), device_id_type=MESH,
        )

    def forward_down(s, y):
        return pltpu.make_async_remote_copy(
            relay.at[s, y - kept], q.at[s, nz, y], z_send.at[1, s, y], z_recv.at[1, s, y],
            device_id=(seam_low, gy), device_id_type=MESH,
        )

    def y_up(s):
        return pltpu.make_async_remote_copy(
            u.at[s, :, ny], u.at[s, :, 0], y_send.at[0, s], y_recv.at[0, s],
            device_id=(gz, gy + 1), device_id_type=MESH,
        )

    def y_down(s):
        return pltpu.make_async_remote_copy(
            v.at[s, :, 0], v.at[s, :, ny], y_send.at[1, s], y_recv.at[1, s],
            device_id=(gz, gy - 1), device_id_type=MESH,
        )

    def send(s, y):
        far = y >= kept
        round_up, round_down = jnp.logical_and(is_low, far), jnp.logical_and(is_high, far)
        pl.when(jnp.logical_and(above, jnp.logical_not(round_up)))(lambda: z_up(s, y).start())
        pl.when(jnp.logical_and(below, jnp.logical_not(round_down)))(lambda: z_down(s, y).start())
        pl.when(round_up)(lambda: relay_up(s, y).start())
        pl.when(round_down)(lambda: relay_down(s, y).start())
        pl.when(jnp.logical_and(y == 0, before))(lambda: y_down(s).start())
        pl.when(jnp.logical_and(y == ny - 1, after))(lambda: y_up(s).start())

    def receive(s, y):
        pl.when(below)(lambda: z_up(s, y).wait_recv())
        pl.when(above)(lambda: z_down(s, y).wait_recv())
        pl.when(jnp.logical_and(y == 0, before))(lambda: y_up(s).wait_recv())
        pl.when(jnp.logical_and(y == ny - 1, after))(lambda: y_down(s).wait_recv())

    def forward(s, y):
        @pl.when(jnp.logical_and(is_last, y < RELAYED))
        def _():
            relay_up(s, y + kept).wait_recv()
            forward_up(s, y + kept).start()

        @pl.when(jnp.logical_and(is_first, y < RELAYED))
        def _():
            relay_down(s, y + kept).wait_recv()
            forward_down(s, y + kept).start()

    small = [
        pltpu.make_async_copy(dirs_hbm, dirs, small_sem.at[0]),
        pltpu.make_async_copy(signs_hbm, signs, small_sem.at[1]),
    ]
    for copy in small:
        copy.start()
    for r in range(ny * nz):
        load(r).start()

    barrier = pltpu.get_barrier_semaphore()
    inner, outer = jnp.logical_or(is_low, is_high), jnp.logical_or(is_first, is_last)
    greeted = [(below, (gz - 1, gy)), (above, (gz + 1, gy)), (before, (gz, gy - 1)), (after, (gz, gy + 1))]
    greeted += [(inner, (0, gy)), (inner, (gz_last, gy)), (outer, (seam_low, gy)), (outer, (seam_high, gy))]
    for there, target in greeted:
        @pl.when(there)
        def _():
            pl.semaphore_signal(barrier, inc=1, device_id=target, device_id_type=MESH)

    @pl.when(gz == 0)
    def _():
        p[:, 0] = jnp.zeros_like(p[:, 0])

    @pl.when(gz == gz_last)
    def _():
        q[:, nz] = jnp.zeros_like(q[:, nz])

    @pl.when(gy == 0)
    def _():
        u[:, :, 0] = jnp.zeros_like(u[:, :, 0])

    @pl.when(gy == gy_last)
    def _():
        v[:, :, ny] = jnp.zeros_like(v[:, :, ny])

    for copy in small:
        copy.wait()
    half_speed = TIME_STEP * jnp.abs(dirs[:, 0:LANES])
    sign = signs[:, 0:LANES].astype(jnp.float32)
    sign_z = sign[2:3]
    rows = [half_speed[0:1], half_speed[1:2], half_speed[2:3]]
    rows.append(1.0 - (rows[0] + rows[1] + rows[2]))
    rows += [sign[0:1] * sign_z, sign[1:2] * sign_z, sign_z]
    table = jnp.concatenate(rows + [jnp.zeros((LANES - len(rows), LANES), jnp.float32)], 0).T
    for c in range(len(rows)):
        coef[c] = jnp.broadcast_to(table[0:HALF, c : c + 1], (HALF, LANES))

    peers = sum(there.astype(jnp.int32) for there, _ in greeted)
    pl.semaphore_wait(barrier, peers)

    def first(y, carry):
        for z in range(nz):
            r = y * nz + z
            load(r).wait()
            for c in range(0, HALF, CHUNK):
                lines = slice(c, c + CHUNK)
                one, other = stage[r, c : c + CHUNK, :], stage[r, HALF + c : HALF + c + CHUNK, :]
                upward, along_y = coef[SZ, lines] > 0, coef[SY, lines] > 0
                up, down = jnp.where(upward, one, other), jnp.where(upward, other, one)
                p[0, z + 1, y, lines] = up
                q[0, z, y, lines] = down
                u[0, z, y + 1, lines] = jnp.where(along_y, up, down)
                v[0, z, y, lines] = jnp.where(along_y, down, up)
        send(0, y)
        return carry

    lax.fori_loop(0, ny, first, 0)

    matrix = angular_matrix(dirs, basis, scaled, left, right)[0:HALF, 0:HALF]
    high = matrix.astype(jnp.bfloat16)
    mat_hi[...] = high
    mat_lo[...] = (matrix - high.astype(jnp.float32)).astype(jnp.bfloat16)

    lane = lax.broadcasted_iota(jnp.int32, (CHUNK, LANES), 1)

    def advance(s, y, last):
        total = jnp.concatenate([p[s, z + 1, y] + q[s, z, y] for z in range(nz)], 1)
        total_hi = total.astype(jnp.bfloat16)
        total_lo = (total - total_hi.astype(jnp.float32)).astype(jnp.bfloat16)
        hi, lo = mat_hi[...], mat_lo[...]
        angular[...] = (
            jnp.dot(hi, total_hi, preferred_element_type=jnp.float32)
            + jnp.dot(hi, total_lo, preferred_element_type=jnp.float32)
            + jnp.dot(lo, total_hi, preferred_element_type=jnp.float32)
        )
        receive(s, y)
        for z in range(nz):
            for c in range(0, HALF, CHUNK):
                lines = slice(c, c + CHUNK)
                up, down = p[s, z + 1, y, lines], q[s, z, y, lines]
                along_x, along_y = coef[SX, lines] > 0, coef[SY, lines] > 0
                rising, falling = jnp.where(along_x, up, down), jnp.where(along_x, down, up)
                rising = jnp.where(lane == 0, 0.0, pltpu.roll(rising, 1, 1))
                falling = jnp.where(lane == LANES - 1, 0.0, pltpu.roll(falling, LANES - 1, 1))
                y_low, y_high = u[s, z, y, lines], v[s, z, y + 1, lines]
                ang = angular[lines, z * LANES : (z + 1) * LANES]
                ax, ay, az, center = (coef[i, lines] for i in (AX, AY, AZ, CENTER))
                new_up = (
                    center * up + ang + ax * jnp.where(along_x, rising, falling)
                    + ay * jnp.where(along_y, y_low, y_high) + az * p[s, z, y, lines]
                )
                new_down = (
                    center * down + ang + ax * jnp.where(along_x, falling, rising)
                    + ay * jnp.where(along_y, y_high, y_low) + az * q[s, z + 1, y, lines]
                )
                if last:
                    r = y * nz + z
                    upward = coef[SZ, lines] > 0
                    stage[r, c : c + CHUNK, :] = jnp.where(upward, new_up, new_down)
                    stage[r, HALF + c : HALF + c + CHUNK, :] = jnp.where(upward, new_down, new_up)
                else:
                    p[s + 1, z + 1, y, lines] = new_up
                    q[s + 1, z, y, lines] = new_down
                    u[s + 1, z, y + 1, lines] = jnp.where(along_y, new_up, new_down)
                    v[s + 1, z, y, lines] = jnp.where(along_y, new_down, new_up)

    def middle(i, carry):
        s, y = i // ny, i % ny
        forward(s, y)
        advance(s, y, False)
        send(s + 1, y)
        return carry

    lax.fori_loop(0, (ITERS - 1) * ny, middle, 0)

    def final(y, carry):
        forward(ITERS - 1, y)
        advance(ITERS - 1, y, True)
        for z in range(nz):
            store(y * nz + z).start()
        return carry

    lax.fori_loop(0, ny, final, 0)

    def sent(i, carry):
        s, y = i // ny, i % ny
        passed = jnp.logical_and(outer, y >= kept)
        pl.when(jnp.logical_or(above, passed))(lambda: z_up(s, y).wait_send())
        pl.when(jnp.logical_or(below, passed))(lambda: z_down(s, y).wait_send())
        return carry

    lax.fori_loop(0, ITERS * ny, sent, 0)
    for s in range(ITERS):
        pl.when(after)(lambda: y_up(s).wait_send())
        pl.when(before)(lambda: y_down(s).wait_send())
    for r in range(ny * nz):
        store(r).wait()


def shards(fodf, directions, signs):
    orientations, ny, nz, _ = fodf.shape
    f32, vmem, dma = jnp.float32, pltpu.VMEM, pltpu.SemaphoreType.DMA
    rows = fodf.reshape(orientations, ny * nz, 1, LANES)
    enhanced = pl.pallas_call(
        kernel,
        out_shape=jax.ShapeDtypeStruct(rows.shape, f32),
        in_specs=[pl.BlockSpec(memory_space=pltpu.HBM)] * 3,
        out_specs=pl.BlockSpec(memory_space=pltpu.HBM),
        scratch_shapes=[
            vmem((ny * nz, orientations, LANES), f32),
            vmem((3, orientations), f32),
            vmem((3, orientations), jnp.int32),
            vmem((7, HALF, LANES), f32),
            vmem((MODES_PAD, LANES), f32),
            vmem((MODES_PAD, LANES), f32),
            vmem((MODES_PAD, LANES), f32),
            vmem((MODES_PAD, LANES), f32),
            vmem((HALF, HALF), jnp.bfloat16),
            vmem((HALF, HALF), jnp.bfloat16),
            vmem((HALF, nz * LANES), f32),
            vmem((ITERS, nz + 1, ny, HALF, LANES), f32),
            vmem((ITERS, nz + 1, ny, HALF, LANES), f32),
            vmem((ITERS, nz, ny + 1, HALF, LANES), f32),
            vmem((ITERS, nz, ny + 1, HALF, LANES), f32),
            vmem((ITERS, RELAYED, HALF, LANES), f32),
            dma((ny * nz,)),
            dma((2,)),
            dma((2, ITERS, ny)),
            dma((2, ITERS, ny)),
            dma((2, ITERS)),
            dma((2, ITERS)),
            dma((ITERS, RELAYED)),
        ],
        compiler_params=pltpu.CompilerParams(
            collective_id=0, has_side_effects=True, vmem_limit_bytes=60 * 1024 * 1024
        ),
    )(rows, directions, signs)
    return enhanced.reshape(fodf.shape)


def solution(mesh):
    placed = (P(None, "gy", "gz", None), P(), P())
    return jax.shard_map(
        shards, mesh=mesh, in_specs=placed, out_specs=P(None, "gy", "gz", None), check_vma=False
    )
```

```python
import math

import jax
import jax.numpy as jnp
from jax import lax
from jax.experimental import pallas as pl
from jax.experimental.pallas import tpu as pltpu
from jax.sharding import PartitionSpec as P

LMAX = 8
ITERS = 4
TIME_STEP = 0.5
DIFFUSION = 0.02

HALF = 96
LANES = 128
MODES = 45
MODES_PAD = 48
CHUNK = 16
RELAYED = 3
HIGHEST = lax.Precision.HIGHEST
MESH = pl.DeviceIdType.MESH

AX, AY, AZ, CENTER, SX, SY, SZ = range(7)


def double_factorial(value):
    result = 1
    while value > 1:
        result = result * value
        value = value - 2
    return result


def harmonic_rows(along_x, along_y, along_z):
    cosines = [jnp.ones_like(along_x)]
    sines = [jnp.zeros_like(along_x)]
    for order in range(1, LMAX + 1):
        cosines.append(cosines[-1] * along_x - sines[-1] * along_y)
        sines.append(cosines[-2] * along_y + sines[-1] * along_x)
    legendre = {}
    for order in range(LMAX + 1):
        legendre[order, order] = double_factorial(2 * order - 1) * jnp.ones_like(along_z)
        if order + 1 <= LMAX:
            legendre[order + 1, order] = (2 * order + 1) * along_z * legendre[order, order]
        for degree in range(order + 2, LMAX + 1):
            legendre[degree, order] = (
                (2 * degree - 1) * along_z * legendre[degree - 1, order]
                - (degree + order - 1) * legendre[degree - 2, order]
            ) * (1.0 / (degree - order))
    rows = []
    for degree in range(0, LMAX + 1, 2):
        for order in range(degree + 1):
            norm = math.sqrt(
                (2 * degree + 1) * math.factorial(degree - order) / math.factorial(degree + order)
            )
            eigenvalue = -float(degree * (degree + 1))
            scaled = norm * legendre[degree, order]
            rows.append((scaled * cosines[order], eigenvalue))
            if order > 0:
                rows.append((scaled * sines[order], eigenvalue))
    return rows


def angular_matrix(dirs, basis, scaled, left, right):
    valid = lax.broadcasted_iota(jnp.int32, (1, LANES), 1) < HALF
    basis[...] = jnp.zeros_like(basis)
    scaled[...] = jnp.zeros_like(scaled)
    left[...] = jnp.zeros_like(left)
    right[...] = jnp.zeros_like(right)
    along = [dirs[a : a + 1, 0:LANES] for a in range(3)]
    for j, (row, eigenvalue) in enumerate(harmonic_rows(*along)):
        row = jnp.where(valid, row, 0.0)
        basis[j : j + 1, :] = row
        scaled[j : j + 1, :] = (TIME_STEP * DIFFUSION * eigenvalue) * row
    b, s = basis[...], scaled[...]
    gram = 2.0 * lax.dot_general(
        b, jnp.concatenate([b, jnp.zeros((LANES - MODES_PAD, LANES), jnp.float32)], 0),
        (((1,), (1,)), ((), ())), precision=HIGHEST, preferred_element_type=jnp.float32,
    )
    index = lax.broadcasted_iota(jnp.int32, (MODES_PAD, LANES), 0)
    for k in range(MODES):
        column = jnp.broadcast_to(gram[:, k : k + 1], (MODES_PAD, LANES))
        inverse = 1.0 / column[k : k + 1, :]
        gram_row, b_row, s_row = gram[k : k + 1, :], b[k : k + 1, :], s[k : k + 1, :]
        left[k : k + 1, :] = s_row
        right[k : k + 1, :] = b_row * inverse
        if k + 1 < MODES:
            factor = jnp.where(index > k, column, 0.0)
            gram = gram - factor * (gram_row * inverse)
            b = b - factor * (b_row * inverse)
            s = s - factor * (s_row * inverse)
    return lax.dot_general(
        left[...].T, right[...], (((1,), (0,)), ((), ())), precision=HIGHEST,
        preferred_element_type=jnp.float32,
    )


def kernel(
    fodf, dirs_hbm, signs_hbm, out,
    stage, dirs, signs, coef, basis, scaled, left, right, mat_hi, mat_lo, angular, p, q, u, v, relay,
    in_sem, small_sem, z_send, z_recv, y_send, y_recv, relay_recv,
):
    ny, nz = p.shape[2], u.shape[1]
    kept = ny - RELAYED
    gz, gy = lax.axis_index("gz"), lax.axis_index("gy")
    gz_last, gy_last = lax.axis_size("gz") - 1, lax.axis_size("gy") - 1
    below, above = gz > 0, gz < gz_last
    before, after = gy > 0, gy < gy_last
    seam_high = (gz_last + 1) // 2
    seam_low = seam_high - 1
    is_low, is_high, is_first, is_last = gz == seam_low, gz == seam_high, gz == 0, gz == gz_last

    def load(r):
        return pltpu.make_async_copy(fodf.at[:, r, 0, :], stage.at[r], in_sem.at[r])

    def z_up(s, y):
        return pltpu.make_async_remote_copy(
            p.at[s, nz, y], p.at[s, 0, y], z_send.at[0, s, y], z_recv.at[0, s, y],
            device_id=(gz + 1, gy), device_id_type=MESH,
        )

    def z_down(s, y):
        return pltpu.make_async_remote_copy(
            q.at[s, 0, y], q.at[s, nz, y], z_send.at[1, s, y], z_recv.at[1, s, y],
            device_id=(gz - 1, gy), device_id_type=MESH,
        )

    def relay_up(s, y):
        return pltpu.make_async_remote_copy(
            p.at[s, nz, y], relay.at[s, y - kept], z_send.at[0, s, y], relay_recv.at[s, y - kept],
            device_id=(0, gy), device_id_type=MESH,
        )

    def relay_down(s, y):
        return pltpu.make_async_remote_copy(
            q.at[s, 0, y], relay.at[s, y - kept], z_send.at[1, s, y], relay_recv.at[s, y - kept],
            device_id=(gz_last, gy), device_id_type=MESH,
        )

    def forward_up(s, y):
        return pltpu.make_async_remote_copy(
            relay.at[s, y - kept], p.at[s, 0, y], z_send.at[1, s, y], z_recv.at[0, s, y],
            device_id=(seam_high, gy), device_id_type=MESH,
        )

    def forward_down(s, y):
        return pltpu.make_async_remote_copy(
            relay.at[s, y - kept], q.at[s, nz, y], z_send.at[0, s, y], z_recv.at[1, s, y],
            device_id=(seam_low, gy), device_id_type=MESH,
        )

    def y_up(s):
        return pltpu.make_async_remote_copy(
            u.at[s, :, ny], u.at[s, :, 0], y_send.at[0, s], y_recv.at[0, s],
            device_id=(gz, gy + 1), device_id_type=MESH,
        )

    def y_down(s):
        return pltpu.make_async_remote_copy(
            v.at[s, :, 0], v.at[s, :, ny], y_send.at[1, s], y_recv.at[1, s],
            device_id=(gz, gy - 1), device_id_type=MESH,
        )

    def send(s, y):
        far = y >= kept
        round_up, round_down = jnp.logical_and(is_low, far), jnp.logical_and(is_high, far)
        pl.when(jnp.logical_and(above, jnp.logical_not(round_up)))(lambda: z_up(s, y).start())
        pl.when(jnp.logical_and(below, jnp.logical_not(round_down)))(lambda: z_down(s, y).start())
        pl.when(round_up)(lambda: relay_up(s, y).start())
        pl.when(round_down)(lambda: relay_down(s, y).start())
        pl.when(jnp.logical_and(y == 0, before))(lambda: y_down(s).start())
        pl.when(jnp.logical_and(y == ny - 1, after))(lambda: y_up(s).start())

    def receive(s, y):
        pl.when(below)(lambda: z_up(s, y).wait_recv())
        pl.when(above)(lambda: z_down(s, y).wait_recv())
        pl.when(jnp.logical_and(y == 0, before))(lambda: y_up(s).wait_recv())
        pl.when(jnp.logical_and(y == ny - 1, after))(lambda: y_down(s).wait_recv())

    def forward(s, y):
        @pl.when(jnp.logical_and(is_first, y < RELAYED))
        def _():
            relay_up(s, y + kept).wait_recv()
            forward_up(s, y + kept).start()

        @pl.when(jnp.logical_and(is_last, y < RELAYED))
        def _():
            relay_down(s, y + kept).wait_recv()
            forward_down(s, y + kept).start()

    small = [
        pltpu.make_async_copy(dirs_hbm, dirs, small_sem.at[0]),
        pltpu.make_async_copy(signs_hbm, signs, small_sem.at[1]),
    ]
    for copy in small:
        copy.start()
    for r in range(ny * nz):
        load(r).start()

    barrier = pltpu.get_barrier_semaphore()
    inner, outer = jnp.logical_or(is_low, is_high), jnp.logical_or(is_first, is_last)
    greeted = [(below, (gz - 1, gy)), (above, (gz + 1, gy)), (before, (gz, gy - 1)), (after, (gz, gy + 1))]
    greeted += [(inner, (0, gy)), (inner, (gz_last, gy)), (outer, (seam_low, gy)), (outer, (seam_high, gy))]
    for there, target in greeted:
        @pl.when(there)
        def _():
            pl.semaphore_signal(barrier, inc=1, device_id=target, device_id_type=MESH)

    @pl.when(gz == 0)
    def _():
        p[:, 0] = jnp.zeros_like(p[:, 0])

    @pl.when(gz == gz_last)
    def _():
        q[:, nz] = jnp.zeros_like(q[:, nz])

    @pl.when(gy == 0)
    def _():
        u[:, :, 0] = jnp.zeros_like(u[:, :, 0])

    @pl.when(gy == gy_last)
    def _():
        v[:, :, ny] = jnp.zeros_like(v[:, :, ny])

    for copy in small:
        copy.wait()
    half_speed = TIME_STEP * jnp.abs(dirs[:, 0:LANES])
    sign = signs[:, 0:LANES].astype(jnp.float32)
    sign_z = sign[2:3]
    rows = [half_speed[0:1], half_speed[1:2], half_speed[2:3]]
    rows.append(1.0 - (rows[0] + rows[1] + rows[2]))
    rows += [sign[0:1] * sign_z, sign[1:2] * sign_z, sign_z]
    table = jnp.concatenate(rows + [jnp.zeros((LANES - len(rows), LANES), jnp.float32)], 0).T
    for c in range(len(rows)):
        coef[c] = jnp.broadcast_to(table[0:HALF, c : c + 1], (HALF, LANES))

    peers = sum(there.astype(jnp.int32) for there, _ in greeted)
    pl.semaphore_wait(barrier, peers)

    def first(y, carry):
        for z in range(nz):
            r = y * nz + z
            load(r).wait()
            for c in range(0, HALF, CHUNK):
                lines = slice(c, c + CHUNK)
                one, other = stage[r, c : c + CHUNK, :], stage[r, HALF + c : HALF + c + CHUNK, :]
                upward, along_y = coef[SZ, lines] > 0, coef[SY, lines] > 0
                up, down = jnp.where(upward, one, other), jnp.where(upward, other, one)
                p[0, z + 1, y, lines] = up
                q[0, z, y, lines] = down
                u[0, z, y + 1, lines] = jnp.where(along_y, up, down)
                v[0, z, y, lines] = jnp.where(along_y, down, up)
        send(0, y)
        return carry

    lax.fori_loop(0, ny, first, 0)

    matrix = angular_matrix(dirs, basis, scaled, left, right)[0:HALF, 0:HALF]
    high = matrix.astype(jnp.bfloat16)
    mat_hi[...] = high
    mat_lo[...] = (matrix - high.astype(jnp.float32)).astype(jnp.bfloat16)

    lane = lax.broadcasted_iota(jnp.int32, (CHUNK, LANES), 1)

    def advance(s, y, last):
        total = jnp.concatenate([p[s, z + 1, y] + q[s, z, y] for z in range(nz)], 1)
        total_hi = total.astype(jnp.bfloat16)
        total_lo = (total - total_hi.astype(jnp.float32)).astype(jnp.bfloat16)
        hi, lo = mat_hi[...], mat_lo[...]
        angular[...] = (
            jnp.dot(hi, total_hi, preferred_element_type=jnp.float32)
            + jnp.dot(hi, total_lo, preferred_element_type=jnp.float32)
            + jnp.dot(lo, total_hi, preferred_element_type=jnp.float32)
        )
        receive(s, y)
        for z in range(nz):
            for c in range(0, HALF, CHUNK):
                lines = slice(c, c + CHUNK)
                up, down = p[s, z + 1, y, lines], q[s, z, y, lines]
                along_x, along_y = coef[SX, lines] > 0, coef[SY, lines] > 0
                rising, falling = jnp.where(along_x, up, down), jnp.where(along_x, down, up)
                rising = jnp.where(lane == 0, 0.0, pltpu.roll(rising, 1, 1))
                falling = jnp.where(lane == LANES - 1, 0.0, pltpu.roll(falling, LANES - 1, 1))
                y_low, y_high = u[s, z, y, lines], v[s, z, y + 1, lines]
                ang = angular[lines, z * LANES : (z + 1) * LANES]
                ax, ay, az, center = (coef[i, lines] for i in (AX, AY, AZ, CENTER))
                new_up = (
                    center * up + ang + ax * jnp.where(along_x, rising, falling)
                    + ay * jnp.where(along_y, y_low, y_high) + az * p[s, z, y, lines]
                )
                new_down = (
                    center * down + ang + ax * jnp.where(along_x, falling, rising)
                    + ay * jnp.where(along_y, y_high, y_low) + az * q[s, z + 1, y, lines]
                )
                if last:
                    r = y * nz + z
                    upward = coef[SZ, lines] > 0
                    one, other = jnp.where(upward, new_up, new_down), jnp.where(upward, new_down, new_up)
                    out[pl.ds(c * ny * nz + r, CHUNK, stride=ny * nz), :] = one
                    out[pl.ds((HALF + c) * ny * nz + r, CHUNK, stride=ny * nz), :] = other
                else:
                    p[s + 1, z + 1, y, lines] = new_up
                    q[s + 1, z, y, lines] = new_down
                    u[s + 1, z, y + 1, lines] = jnp.where(along_y, new_up, new_down)
                    v[s + 1, z, y, lines] = jnp.where(along_y, new_down, new_up)

    def middle(i, carry):
        s, y = i // ny, i % ny
        forward(s, y)
        advance(s, y, False)
        send(s + 1, y)
        return carry

    lax.fori_loop(0, (ITERS - 1) * ny, middle, 0)

    def final(y, carry):
        forward(ITERS - 1, y)
        advance(ITERS - 1, y, True)
        return carry

    lax.fori_loop(0, ny, final, 0)

    def sent(i, carry):
        s, y = i // ny, i % ny
        passed = jnp.logical_and(outer, y >= kept)
        pl.when(jnp.logical_or(above, passed))(lambda: z_up(s, y).wait_send())
        pl.when(jnp.logical_or(below, passed))(lambda: z_down(s, y).wait_send())
        return carry

    lax.fori_loop(0, ITERS * ny, sent, 0)
    for s in range(ITERS):
        pl.when(after)(lambda: y_up(s).wait_send())
        pl.when(before)(lambda: y_down(s).wait_send())


def shards(fodf, directions, signs):
    orientations, ny, nz, _ = fodf.shape
    f32, vmem, dma = jnp.float32, pltpu.VMEM, pltpu.SemaphoreType.DMA
    rows = fodf.reshape(orientations, ny * nz, 1, LANES)
    enhanced = pl.pallas_call(
        kernel,
        out_shape=vmem((orientations * ny * nz, LANES), f32),
        in_specs=[pl.BlockSpec(memory_space=pltpu.HBM)] * 3,
        out_specs=pl.BlockSpec(memory_space=vmem),
        scratch_shapes=[
            vmem((ny * nz, orientations, LANES), f32),
            vmem((3, orientations), f32),
            vmem((3, orientations), jnp.int32),
            vmem((7, HALF, LANES), f32),
            vmem((MODES_PAD, LANES), f32),
            vmem((MODES_PAD, LANES), f32),
            vmem((MODES_PAD, LANES), f32),
            vmem((MODES_PAD, LANES), f32),
            vmem((HALF, HALF), jnp.bfloat16),
            vmem((HALF, HALF), jnp.bfloat16),
            vmem((HALF, nz * LANES), f32),
            vmem((ITERS, nz + 1, ny, HALF, LANES), f32),
            vmem((ITERS, nz + 1, ny, HALF, LANES), f32),
            vmem((ITERS, nz, ny + 1, HALF, LANES), f32),
            vmem((ITERS, nz, ny + 1, HALF, LANES), f32),
            vmem((ITERS, RELAYED, HALF, LANES), f32),
            dma((ny * nz,)),
            dma((2,)),
            dma((2, ITERS, ny)),
            dma((2, ITERS, ny)),
            dma((2, ITERS)),
            dma((2, ITERS)),
            dma((ITERS, RELAYED)),
        ],
        compiler_params=pltpu.CompilerParams(
            collective_id=0, has_side_effects=True, vmem_limit_bytes=48 * 1024 * 1024
        ),
    )(*(pltpu.with_memory_space_constraint(a, pltpu.HBM) for a in (rows, directions, signs)))
    return enhanced.reshape(fodf.shape)


def solution(mesh):
    placed = (P(None, "gy", "gz", None), P(), P())
    return jax.shard_map(
        shards, mesh=mesh, in_specs=placed, out_specs=P(None, "gy", "gz", None), check_vma=False
    )
```

```python
import math

import jax
import jax.numpy as jnp
from jax import lax
from jax.experimental import pallas as pl
from jax.experimental.pallas import tpu as pltpu
from jax.sharding import PartitionSpec as P

LMAX = 8
ITERS = 4
TIME_STEP = 0.5
DIFFUSION = 0.02

HALF = 96
LANES = 128
MODES = 45
MODES_PAD = 48
CHUNK = 16
RELAYED = 3
HIGHEST = lax.Precision.HIGHEST
MESH = pl.DeviceIdType.MESH

AX, AY, AZ, CENTER, SX, SY, SZ = range(7)


def double_factorial(value):
    result = 1
    while value > 1:
        result = result * value
        value = value - 2
    return result


def harmonic_rows(along_x, along_y, along_z):
    cosines = [jnp.ones_like(along_x)]
    sines = [jnp.zeros_like(along_x)]
    for order in range(1, LMAX + 1):
        cosines.append(cosines[-1] * along_x - sines[-1] * along_y)
        sines.append(cosines[-2] * along_y + sines[-1] * along_x)
    legendre = {}
    for order in range(LMAX + 1):
        legendre[order, order] = double_factorial(2 * order - 1) * jnp.ones_like(along_z)
        if order + 1 <= LMAX:
            legendre[order + 1, order] = (2 * order + 1) * along_z * legendre[order, order]
        for degree in range(order + 2, LMAX + 1):
            legendre[degree, order] = (
                (2 * degree - 1) * along_z * legendre[degree - 1, order]
                - (degree + order - 1) * legendre[degree - 2, order]
            ) * (1.0 / (degree - order))
    rows = []
    for degree in range(0, LMAX + 1, 2):
        for order in range(degree + 1):
            norm = math.sqrt(
                (2 * degree + 1) * math.factorial(degree - order) / math.factorial(degree + order)
            )
            eigenvalue = -float(degree * (degree + 1))
            scaled = norm * legendre[degree, order]
            rows.append((scaled * cosines[order], eigenvalue))
            if order > 0:
                rows.append((scaled * sines[order], eigenvalue))
    return rows


def angular_matrix(dirs, basis, scaled, left, right):
    valid = lax.broadcasted_iota(jnp.int32, (1, LANES), 1) < HALF
    basis[...] = jnp.zeros_like(basis)
    scaled[...] = jnp.zeros_like(scaled)
    left[...] = jnp.zeros_like(left)
    right[...] = jnp.zeros_like(right)
    along = [dirs[a : a + 1, 0:LANES] for a in range(3)]
    for j, (row, eigenvalue) in enumerate(harmonic_rows(*along)):
        row = jnp.where(valid, row, 0.0)
        basis[j : j + 1, :] = row
        scaled[j : j + 1, :] = (TIME_STEP * DIFFUSION * eigenvalue) * row
    b, s = basis[...], scaled[...]
    gram = 2.0 * lax.dot_general(
        b, jnp.concatenate([b, jnp.zeros((LANES - MODES_PAD, LANES), jnp.float32)], 0),
        (((1,), (1,)), ((), ())), precision=HIGHEST, preferred_element_type=jnp.float32,
    )
    index = lax.broadcasted_iota(jnp.int32, (MODES_PAD, LANES), 0)
    for k in range(MODES):
        column = jnp.broadcast_to(gram[:, k : k + 1], (MODES_PAD, LANES))
        inverse = 1.0 / column[k : k + 1, :]
        gram_row, b_row, s_row = gram[k : k + 1, :], b[k : k + 1, :], s[k : k + 1, :]
        left[k : k + 1, :] = s_row
        right[k : k + 1, :] = b_row * inverse
        if k + 1 < MODES:
            factor = jnp.where(index > k, column, 0.0)
            gram = gram - factor * (gram_row * inverse)
            b = b - factor * (b_row * inverse)
            s = s - factor * (s_row * inverse)
    return lax.dot_general(
        left[...].T, right[...], (((1,), (0,)), ((), ())), precision=HIGHEST,
        preferred_element_type=jnp.float32,
    )


def kernel(
    fodf, dirs_hbm, signs_hbm, out,
    stage, dirs, signs, coef, basis, scaled, left, right, mat_hi, mat_lo, angular, p, q, u, v, relay,
    in_sem, small_sem, z_send, z_recv, y_send, y_recv, relay_recv,
):
    ny, nz = p.shape[2], u.shape[1]
    kept = ny - RELAYED

    def row_at(i):
        return (i + ny - 1) % ny

    gz, gy = lax.axis_index("gz"), lax.axis_index("gy")
    gz_last, gy_last = lax.axis_size("gz") - 1, lax.axis_size("gy") - 1
    below, above = gz > 0, gz < gz_last
    before, after = gy > 0, gy < gy_last
    seam_high = (gz_last + 1) // 2
    seam_low = seam_high - 1
    is_low, is_high, is_first, is_last = gz == seam_low, gz == seam_high, gz == 0, gz == gz_last

    def load(r):
        return pltpu.make_async_copy(fodf.at[:, r, 0, :], stage.at[r], in_sem.at[r])

    def z_up(s, y):
        return pltpu.make_async_remote_copy(
            p.at[s, nz, y], p.at[s, 0, y], z_send.at[0, s, y], z_recv.at[0, s, y],
            device_id=(gz + 1, gy), device_id_type=MESH,
        )

    def z_down(s, y):
        return pltpu.make_async_remote_copy(
            q.at[s, 0, y], q.at[s, nz, y], z_send.at[1, s, y], z_recv.at[1, s, y],
            device_id=(gz - 1, gy), device_id_type=MESH,
        )

    def relay_up(s, i):
        return pltpu.make_async_remote_copy(
            p.at[s, nz, row_at(i)], relay.at[s, i - kept], z_send.at[0, s, row_at(i)], relay_recv.at[s, i - kept],
            device_id=(0, gy), device_id_type=MESH,
        )

    def relay_down(s, i):
        return pltpu.make_async_remote_copy(
            q.at[s, 0, row_at(i)], relay.at[s, i - kept], z_send.at[1, s, row_at(i)], relay_recv.at[s, i - kept],
            device_id=(gz_last, gy), device_id_type=MESH,
        )

    def forward_up(s, i):
        return pltpu.make_async_remote_copy(
            relay.at[s, i - kept], p.at[s, 0, row_at(i)], z_send.at[1, s, row_at(i)], z_recv.at[0, s, row_at(i)],
            device_id=(seam_high, gy), device_id_type=MESH,
        )

    def forward_down(s, i):
        return pltpu.make_async_remote_copy(
            relay.at[s, i - kept], q.at[s, nz, row_at(i)], z_send.at[0, s, row_at(i)], z_recv.at[1, s, row_at(i)],
            device_id=(seam_low, gy), device_id_type=MESH,
        )

    def y_up(s):
        return pltpu.make_async_remote_copy(
            u.at[s, :, ny], u.at[s, :, 0], y_send.at[0, s], y_recv.at[0, s],
            device_id=(gz, gy + 1), device_id_type=MESH,
        )

    def y_down(s):
        return pltpu.make_async_remote_copy(
            v.at[s, :, 0], v.at[s, :, ny], y_send.at[1, s], y_recv.at[1, s],
            device_id=(gz, gy - 1), device_id_type=MESH,
        )

    def send(s, i):
        y, far = row_at(i), i >= kept
        round_up, round_down = jnp.logical_and(is_low, far), jnp.logical_and(is_high, far)
        pl.when(jnp.logical_and(above, jnp.logical_not(round_up)))(lambda: z_up(s, y).start())
        pl.when(jnp.logical_and(below, jnp.logical_not(round_down)))(lambda: z_down(s, y).start())
        pl.when(round_up)(lambda: relay_up(s, i).start())
        pl.when(round_down)(lambda: relay_down(s, i).start())
        pl.when(jnp.logical_and(y == 0, before))(lambda: y_down(s).start())
        pl.when(jnp.logical_and(y == ny - 1, after))(lambda: y_up(s).start())

    def receive(s, y):
        pl.when(below)(lambda: z_up(s, y).wait_recv())
        pl.when(above)(lambda: z_down(s, y).wait_recv())
        pl.when(jnp.logical_and(y == 0, before))(lambda: y_up(s).wait_recv())
        pl.when(jnp.logical_and(y == ny - 1, after))(lambda: y_down(s).wait_recv())

    def forward(s, i):
        @pl.when(jnp.logical_and(is_first, i < RELAYED))
        def _():
            relay_up(s, i + kept).wait_recv()
            forward_up(s, i + kept).start()

        @pl.when(jnp.logical_and(is_last, i < RELAYED))
        def _():
            relay_down(s, i + kept).wait_recv()
            forward_down(s, i + kept).start()

    small = [
        pltpu.make_async_copy(dirs_hbm, dirs, small_sem.at[0]),
        pltpu.make_async_copy(signs_hbm, signs, small_sem.at[1]),
    ]
    for copy in small:
        copy.start()
    for i in range(ny):
        for z in range(nz):
            load(row_at(i) * nz + z).start()

    barrier = pltpu.get_barrier_semaphore()
    inner, outer = jnp.logical_or(is_low, is_high), jnp.logical_or(is_first, is_last)
    greeted = [(below, (gz - 1, gy)), (above, (gz + 1, gy)), (before, (gz, gy - 1)), (after, (gz, gy + 1))]
    greeted += [(inner, (0, gy)), (inner, (gz_last, gy)), (outer, (seam_low, gy)), (outer, (seam_high, gy))]
    for there, target in greeted:
        @pl.when(there)
        def _():
            pl.semaphore_signal(barrier, inc=1, device_id=target, device_id_type=MESH)

    @pl.when(gz == 0)
    def _():
        p[:, 0] = jnp.zeros_like(p[:, 0])

    @pl.when(gz == gz_last)
    def _():
        q[:, nz] = jnp.zeros_like(q[:, nz])

    @pl.when(gy == 0)
    def _():
        u[:, :, 0] = jnp.zeros_like(u[:, :, 0])

    @pl.when(gy == gy_last)
    def _():
        v[:, :, ny] = jnp.zeros_like(v[:, :, ny])

    for copy in small:
        copy.wait()
    half_speed = TIME_STEP * jnp.abs(dirs[:, 0:LANES])
    sign = signs[:, 0:LANES].astype(jnp.float32)
    sign_z = sign[2:3]
    rows = [half_speed[0:1], half_speed[1:2], half_speed[2:3]]
    rows.append(1.0 - (rows[0] + rows[1] + rows[2]))
    rows += [sign[0:1] * sign_z, sign[1:2] * sign_z, sign_z]
    table = jnp.concatenate(rows + [jnp.zeros((LANES - len(rows), LANES), jnp.float32)], 0).T
    for c in range(len(rows)):
        coef[c] = jnp.broadcast_to(table[0:HALF, c : c + 1], (HALF, LANES))

    peers = sum(there.astype(jnp.int32) for there, _ in greeted)
    pl.semaphore_wait(barrier, peers)

    def first(i, carry):
        y = row_at(i)
        for z in range(nz):
            r = y * nz + z
            load(r).wait()
            for c in range(0, HALF, CHUNK):
                lines = slice(c, c + CHUNK)
                one, other = stage[r, c : c + CHUNK, :], stage[r, HALF + c : HALF + c + CHUNK, :]
                upward, along_y = coef[SZ, lines] > 0, coef[SY, lines] > 0
                up, down = jnp.where(upward, one, other), jnp.where(upward, other, one)
                p[0, z + 1, y, lines] = up
                q[0, z, y, lines] = down
                u[0, z, y + 1, lines] = jnp.where(along_y, up, down)
                v[0, z, y, lines] = jnp.where(along_y, down, up)
        send(0, i)
        return carry

    lax.fori_loop(0, ny, first, 0)

    matrix = angular_matrix(dirs, basis, scaled, left, right)[0:HALF, 0:HALF]
    high = matrix.astype(jnp.bfloat16)
    mat_hi[...] = high
    mat_lo[...] = (matrix - high.astype(jnp.float32)).astype(jnp.bfloat16)

    lane = lax.broadcasted_iota(jnp.int32, (CHUNK, LANES), 1)

    def advance(s, y, last):
        total = jnp.concatenate([p[s, z + 1, y] + q[s, z, y] for z in range(nz)], 1)
        total_hi = total.astype(jnp.bfloat16)
        total_lo = (total - total_hi.astype(jnp.float32)).astype(jnp.bfloat16)
        hi, lo = mat_hi[...], mat_lo[...]
        angular[...] = (
            jnp.dot(hi, total_hi, preferred_element_type=jnp.float32)
            + jnp.dot(hi, total_lo, preferred_element_type=jnp.float32)
            + jnp.dot(lo, total_hi, preferred_element_type=jnp.float32)
        )
        receive(s, y)
        for z in range(nz):
            for c in range(0, HALF, CHUNK):
                lines = slice(c, c + CHUNK)
                up, down = p[s, z + 1, y, lines], q[s, z, y, lines]
                along_x, along_y = coef[SX, lines] > 0, coef[SY, lines] > 0
                rising, falling = jnp.where(along_x, up, down), jnp.where(along_x, down, up)
                rising = jnp.where(lane == 0, 0.0, pltpu.roll(rising, 1, 1))
                falling = jnp.where(lane == LANES - 1, 0.0, pltpu.roll(falling, LANES - 1, 1))
                y_low, y_high = u[s, z, y, lines], v[s, z, y + 1, lines]
                ang = angular[lines, z * LANES : (z + 1) * LANES]
                ax, ay, az, center = (coef[i, lines] for i in (AX, AY, AZ, CENTER))
                new_up = (
                    center * up + ang + ax * jnp.where(along_x, rising, falling)
                    + ay * jnp.where(along_y, y_low, y_high) + az * p[s, z, y, lines]
                )
                new_down = (
                    center * down + ang + ax * jnp.where(along_x, falling, rising)
                    + ay * jnp.where(along_y, y_high, y_low) + az * q[s, z + 1, y, lines]
                )
                if last:
                    r = y * nz + z
                    upward = coef[SZ, lines] > 0
                    one, other = jnp.where(upward, new_up, new_down), jnp.where(upward, new_down, new_up)
                    out[pl.ds(c * ny * nz + r, CHUNK, stride=ny * nz), :] = one
                    out[pl.ds((HALF + c) * ny * nz + r, CHUNK, stride=ny * nz), :] = other
                else:
                    p[s + 1, z + 1, y, lines] = new_up
                    q[s + 1, z, y, lines] = new_down
                    u[s + 1, z, y + 1, lines] = jnp.where(along_y, new_up, new_down)
                    v[s + 1, z, y, lines] = jnp.where(along_y, new_down, new_up)

    def middle(n, carry):
        s, i = n // ny, n % ny
        forward(s, i)
        advance(s, row_at(i), False)
        send(s + 1, i)
        return carry

    lax.fori_loop(0, (ITERS - 1) * ny, middle, 0)

    def final(i, carry):
        forward(ITERS - 1, i)
        advance(ITERS - 1, row_at(i), True)
        return carry

    lax.fori_loop(0, ny, final, 0)

    def sent(n, carry):
        s, i = n // ny, n % ny
        y, passed = row_at(i), jnp.logical_and(outer, i >= kept)
        pl.when(jnp.logical_or(above, passed))(lambda: z_up(s, y).wait_send())
        pl.when(jnp.logical_or(below, passed))(lambda: z_down(s, y).wait_send())
        return carry

    lax.fori_loop(0, ITERS * ny, sent, 0)
    for s in range(ITERS):
        pl.when(after)(lambda: y_up(s).wait_send())
        pl.when(before)(lambda: y_down(s).wait_send())


def shards(fodf, directions, signs):
    orientations, ny, nz, _ = fodf.shape
    f32, vmem, dma = jnp.float32, pltpu.VMEM, pltpu.SemaphoreType.DMA
    rows = fodf.reshape(orientations, ny * nz, 1, LANES)
    enhanced = pl.pallas_call(
        kernel,
        out_shape=vmem((orientations * ny * nz, LANES), f32),
        in_specs=[pl.BlockSpec(memory_space=pltpu.HBM)] * 3,
        out_specs=pl.BlockSpec(memory_space=vmem),
        scratch_shapes=[
            vmem((ny * nz, orientations, LANES), f32),
            vmem((3, orientations), f32),
            vmem((3, orientations), jnp.int32),
            vmem((7, HALF, LANES), f32),
            vmem((MODES_PAD, LANES), f32),
            vmem((MODES_PAD, LANES), f32),
            vmem((MODES_PAD, LANES), f32),
            vmem((MODES_PAD, LANES), f32),
            vmem((HALF, HALF), jnp.bfloat16),
            vmem((HALF, HALF), jnp.bfloat16),
            vmem((HALF, nz * LANES), f32),
            vmem((ITERS, nz + 1, ny, HALF, LANES), f32),
            vmem((ITERS, nz + 1, ny, HALF, LANES), f32),
            vmem((ITERS, nz, ny + 1, HALF, LANES), f32),
            vmem((ITERS, nz, ny + 1, HALF, LANES), f32),
            vmem((ITERS, RELAYED, HALF, LANES), f32),
            dma((ny * nz,)),
            dma((2,)),
            dma((2, ITERS, ny)),
            dma((2, ITERS, ny)),
            dma((2, ITERS)),
            dma((2, ITERS)),
            dma((ITERS, RELAYED)),
        ],
        compiler_params=pltpu.CompilerParams(
            collective_id=0, has_side_effects=True, vmem_limit_bytes=48 * 1024 * 1024
        ),
    )(*(pltpu.with_memory_space_constraint(a, pltpu.HBM) for a in (rows, directions, signs)))
    return enhanced.reshape(fodf.shape)


def solution(mesh):
    placed = (P(None, "gy", "gz", None), P(), P())
    return jax.shard_map(
        shards, mesh=mesh, in_specs=placed, out_specs=P(None, "gy", "gz", None), check_vma=False
    )
```

```python
import math

import jax
import jax.numpy as jnp
from jax import lax
from jax.experimental import pallas as pl
from jax.experimental.pallas import tpu as pltpu
from jax.sharding import PartitionSpec as P

LMAX = 8
ITERS = 4
TIME_STEP = 0.5
DIFFUSION = 0.02

HALF = 96
LANES = 128
MODES = 45
MODES_PAD = 48
CHUNK = 16
RELAYED = 3
HIGHEST = lax.Precision.HIGHEST
MESH = pl.DeviceIdType.MESH

AX, AY, AZ, CENTER, SX, SY, SZ = range(7)


def double_factorial(value):
    result = 1
    while value > 1:
        result = result * value
        value = value - 2
    return result


def harmonic_rows(along_x, along_y, along_z):
    cosines = [jnp.ones_like(along_x)]
    sines = [jnp.zeros_like(along_x)]
    for order in range(1, LMAX + 1):
        cosines.append(cosines[-1] * along_x - sines[-1] * along_y)
        sines.append(cosines[-2] * along_y + sines[-1] * along_x)
    legendre = {}
    for order in range(LMAX + 1):
        legendre[order, order] = double_factorial(2 * order - 1) * jnp.ones_like(along_z)
        if order + 1 <= LMAX:
            legendre[order + 1, order] = (2 * order + 1) * along_z * legendre[order, order]
        for degree in range(order + 2, LMAX + 1):
            legendre[degree, order] = (
                (2 * degree - 1) * along_z * legendre[degree - 1, order]
                - (degree + order - 1) * legendre[degree - 2, order]
            ) * (1.0 / (degree - order))
    rows = []
    for degree in range(0, LMAX + 1, 2):
        for order in range(degree + 1):
            norm = math.sqrt(
                (2 * degree + 1) * math.factorial(degree - order) / math.factorial(degree + order)
            )
            eigenvalue = -float(degree * (degree + 1))
            scaled = norm * legendre[degree, order]
            rows.append((scaled * cosines[order], eigenvalue))
            if order > 0:
                rows.append((scaled * sines[order], eigenvalue))
    return rows


def angular_matrix(dirs, basis, scaled, left, right):
    valid = lax.broadcasted_iota(jnp.int32, (1, LANES), 1) < HALF
    basis[...] = jnp.zeros_like(basis)
    scaled[...] = jnp.zeros_like(scaled)
    left[...] = jnp.zeros_like(left)
    right[...] = jnp.zeros_like(right)
    along = [dirs[a : a + 1, 0:LANES] for a in range(3)]
    for j, (row, eigenvalue) in enumerate(harmonic_rows(*along)):
        row = jnp.where(valid, row, 0.0)
        basis[j : j + 1, :] = row
        scaled[j : j + 1, :] = (TIME_STEP * DIFFUSION * eigenvalue) * row
    b, s = basis[...], scaled[...]
    gram = 2.0 * lax.dot_general(
        b, jnp.concatenate([b, jnp.zeros((LANES - MODES_PAD, LANES), jnp.float32)], 0),
        (((1,), (1,)), ((), ())), precision=HIGHEST, preferred_element_type=jnp.float32,
    )
    index = lax.broadcasted_iota(jnp.int32, (MODES_PAD, LANES), 0)
    for k in range(MODES):
        column = jnp.broadcast_to(gram[:, k : k + 1], (MODES_PAD, LANES))
        inverse = 1.0 / column[k : k + 1, :]
        gram_row, b_row, s_row = gram[k : k + 1, :], b[k : k + 1, :], s[k : k + 1, :]
        left[k : k + 1, :] = s_row
        right[k : k + 1, :] = b_row * inverse
        if k + 1 < MODES:
            factor = jnp.where(index > k, column, 0.0)
            gram = gram - factor * (gram_row * inverse)
            b = b - factor * (b_row * inverse)
            s = s - factor * (s_row * inverse)
    return lax.dot_general(
        left[...].T, right[...], (((1,), (0,)), ((), ())), precision=HIGHEST,
        preferred_element_type=jnp.float32,
    )


def kernel(
    fodf, dirs_hbm, signs_hbm, out,
    stage, dirs, signs, coef, basis, scaled, left, right, mat_hi, mat_lo, angular, p, q, u, v, relay,
    in_sem, small_sem, z_send, z_recv, y_send, y_recv, relay_recv,
):
    ny, nz = p.shape[2], u.shape[1]

    def row_at(i):
        return (i + ny - 1) % ny

    gz, gy = lax.axis_index("gz"), lax.axis_index("gy")
    gz_last, gy_last = lax.axis_size("gz") - 1, lax.axis_size("gy") - 1
    below, above = gz > 0, gz < gz_last
    before, after = gy > 0, gy < gy_last
    seam_high = (gz_last + 1) // 2
    seam_low = seam_high - 1
    is_low, is_high, is_first, is_last = gz == seam_low, gz == seam_high, gz == 0, gz == gz_last

    def load(r):
        return pltpu.make_async_copy(fodf.at[:, r, 0, :], stage.at[r], in_sem.at[r])

    def z_up(s, y):
        return pltpu.make_async_remote_copy(
            p.at[s, nz, y], p.at[s, 0, y], z_send.at[0, s, y], z_recv.at[0, s, y],
            device_id=(gz + 1, gy), device_id_type=MESH,
        )

    def z_down(s, y):
        return pltpu.make_async_remote_copy(
            q.at[s, 0, y], q.at[s, nz, y], z_send.at[1, s, y], z_recv.at[1, s, y],
            device_id=(gz - 1, gy), device_id_type=MESH,
        )

    def relay_up(s, i):
        return pltpu.make_async_remote_copy(
            p.at[s, nz, row_at(i)], relay.at[s, i], z_send.at[0, s, row_at(i)], relay_recv.at[s, i],
            device_id=(0, gy), device_id_type=MESH,
        )

    def relay_down(s, i):
        return pltpu.make_async_remote_copy(
            q.at[s, 0, row_at(i)], relay.at[s, i], z_send.at[1, s, row_at(i)], relay_recv.at[s, i],
            device_id=(gz_last, gy), device_id_type=MESH,
        )

    def forward_up(s, i):
        return pltpu.make_async_remote_copy(
            relay.at[s, i], p.at[s, 0, row_at(i)], z_send.at[1, s, row_at(i)], z_recv.at[0, s, row_at(i)],
            device_id=(seam_high, gy), device_id_type=MESH,
        )

    def forward_down(s, i):
        return pltpu.make_async_remote_copy(
            relay.at[s, i], q.at[s, nz, row_at(i)], z_send.at[0, s, row_at(i)], z_recv.at[1, s, row_at(i)],
            device_id=(seam_low, gy), device_id_type=MESH,
        )

    def y_up(s):
        return pltpu.make_async_remote_copy(
            u.at[s, :, ny], u.at[s, :, 0], y_send.at[0, s], y_recv.at[0, s],
            device_id=(gz, gy + 1), device_id_type=MESH,
        )

    def y_down(s):
        return pltpu.make_async_remote_copy(
            v.at[s, :, 0], v.at[s, :, ny], y_send.at[1, s], y_recv.at[1, s],
            device_id=(gz, gy - 1), device_id_type=MESH,
        )

    def send(s, i):
        y, far = row_at(i), i < RELAYED
        round_up, round_down = jnp.logical_and(is_low, far), jnp.logical_and(is_high, far)
        pl.when(jnp.logical_and(above, jnp.logical_not(round_up)))(lambda: z_up(s, y).start())
        pl.when(jnp.logical_and(below, jnp.logical_not(round_down)))(lambda: z_down(s, y).start())
        pl.when(round_up)(lambda: relay_up(s, i).start())
        pl.when(round_down)(lambda: relay_down(s, i).start())
        pl.when(jnp.logical_and(y == 0, before))(lambda: y_down(s).start())
        pl.when(jnp.logical_and(y == ny - 1, after))(lambda: y_up(s).start())

    def receive(s, y):
        pl.when(below)(lambda: z_up(s, y).wait_recv())
        pl.when(above)(lambda: z_down(s, y).wait_recv())
        pl.when(jnp.logical_and(y == 0, before))(lambda: y_up(s).wait_recv())
        pl.when(jnp.logical_and(y == ny - 1, after))(lambda: y_down(s).wait_recv())

    def forward(s, i):
        @pl.when(is_first)
        def _():
            relay_up(s, i).wait_recv()
            forward_up(s, i).start()

        @pl.when(is_last)
        def _():
            relay_down(s, i).wait_recv()
            forward_down(s, i).start()

    small = [
        pltpu.make_async_copy(dirs_hbm, dirs, small_sem.at[0]),
        pltpu.make_async_copy(signs_hbm, signs, small_sem.at[1]),
    ]
    for copy in small:
        copy.start()
    for i in range(ny):
        for z in range(nz):
            load(row_at(i) * nz + z).start()

    barrier = pltpu.get_barrier_semaphore()
    inner, outer = jnp.logical_or(is_low, is_high), jnp.logical_or(is_first, is_last)
    greeted = [(below, (gz - 1, gy)), (above, (gz + 1, gy)), (before, (gz, gy - 1)), (after, (gz, gy + 1))]
    greeted += [(inner, (0, gy)), (inner, (gz_last, gy)), (outer, (seam_low, gy)), (outer, (seam_high, gy))]
    for there, target in greeted:
        @pl.when(there)
        def _():
            pl.semaphore_signal(barrier, inc=1, device_id=target, device_id_type=MESH)

    @pl.when(gz == 0)
    def _():
        p[:, 0] = jnp.zeros_like(p[:, 0])

    @pl.when(gz == gz_last)
    def _():
        q[:, nz] = jnp.zeros_like(q[:, nz])

    @pl.when(gy == 0)
    def _():
        u[:, :, 0] = jnp.zeros_like(u[:, :, 0])

    @pl.when(gy == gy_last)
    def _():
        v[:, :, ny] = jnp.zeros_like(v[:, :, ny])

    for copy in small:
        copy.wait()
    half_speed = TIME_STEP * jnp.abs(dirs[:, 0:LANES])
    sign = signs[:, 0:LANES].astype(jnp.float32)
    sign_z = sign[2:3]
    rows = [half_speed[0:1], half_speed[1:2], half_speed[2:3]]
    rows.append(1.0 - (rows[0] + rows[1] + rows[2]))
    rows += [sign[0:1] * sign_z, sign[1:2] * sign_z, sign_z]
    table = jnp.concatenate(rows + [jnp.zeros((LANES - len(rows), LANES), jnp.float32)], 0).T
    for c in range(len(rows)):
        coef[c] = jnp.broadcast_to(table[0:HALF, c : c + 1], (HALF, LANES))

    peers = sum(there.astype(jnp.int32) for there, _ in greeted)
    pl.semaphore_wait(barrier, peers)

    def first(i, carry):
        y = row_at(i)
        for z in range(nz):
            r = y * nz + z
            load(r).wait()
            for c in range(0, HALF, CHUNK):
                lines = slice(c, c + CHUNK)
                one, other = stage[r, c : c + CHUNK, :], stage[r, HALF + c : HALF + c + CHUNK, :]
                upward, along_y = coef[SZ, lines] > 0, coef[SY, lines] > 0
                up, down = jnp.where(upward, one, other), jnp.where(upward, other, one)
                p[0, z + 1, y, lines] = up
                q[0, z, y, lines] = down
                u[0, z, y + 1, lines] = jnp.where(along_y, up, down)
                v[0, z, y, lines] = jnp.where(along_y, down, up)
        send(0, i)
        return carry

    lax.fori_loop(0, ny, first, 0)

    matrix = angular_matrix(dirs, basis, scaled, left, right)[0:HALF, 0:HALF]
    high = matrix.astype(jnp.bfloat16)
    mat_hi[...] = high
    mat_lo[...] = (matrix - high.astype(jnp.float32)).astype(jnp.bfloat16)

    lane = lax.broadcasted_iota(jnp.int32, (CHUNK, LANES), 1)

    def advance(s, y, last):
        total = jnp.concatenate([p[s, z + 1, y] + q[s, z, y] for z in range(nz)], 1)
        total_hi = total.astype(jnp.bfloat16)
        total_lo = (total - total_hi.astype(jnp.float32)).astype(jnp.bfloat16)
        hi, lo = mat_hi[...], mat_lo[...]
        angular[...] = (
            jnp.dot(hi, total_hi, preferred_element_type=jnp.float32)
            + jnp.dot(hi, total_lo, preferred_element_type=jnp.float32)
            + jnp.dot(lo, total_hi, preferred_element_type=jnp.float32)
        )
        receive(s, y)
        for z in range(nz):
            for c in range(0, HALF, CHUNK):
                lines = slice(c, c + CHUNK)
                up, down = p[s, z + 1, y, lines], q[s, z, y, lines]
                along_x, along_y = coef[SX, lines] > 0, coef[SY, lines] > 0
                rising, falling = jnp.where(along_x, up, down), jnp.where(along_x, down, up)
                rising = jnp.where(lane == 0, 0.0, pltpu.roll(rising, 1, 1))
                falling = jnp.where(lane == LANES - 1, 0.0, pltpu.roll(falling, LANES - 1, 1))
                y_low, y_high = u[s, z, y, lines], v[s, z, y + 1, lines]
                ang = angular[lines, z * LANES : (z + 1) * LANES]
                ax, ay, az, center = (coef[i, lines] for i in (AX, AY, AZ, CENTER))
                new_up = (
                    center * up + ang + ax * jnp.where(along_x, rising, falling)
                    + ay * jnp.where(along_y, y_low, y_high) + az * p[s, z, y, lines]
                )
                new_down = (
                    center * down + ang + ax * jnp.where(along_x, falling, rising)
                    + ay * jnp.where(along_y, y_high, y_low) + az * q[s, z + 1, y, lines]
                )
                if last:
                    r = y * nz + z
                    upward = coef[SZ, lines] > 0
                    one, other = jnp.where(upward, new_up, new_down), jnp.where(upward, new_down, new_up)
                    out[pl.ds(c * ny * nz + r, CHUNK, stride=ny * nz), :] = one
                    out[pl.ds((HALF + c) * ny * nz + r, CHUNK, stride=ny * nz), :] = other
                else:
                    p[s + 1, z + 1, y, lines] = new_up
                    q[s + 1, z, y, lines] = new_down
                    u[s + 1, z, y + 1, lines] = jnp.where(along_y, new_up, new_down)
                    v[s + 1, z, y, lines] = jnp.where(along_y, new_down, new_up)

    def middle(n, carry):
        s, i = n // ny, n % ny
        advance(s, row_at(i), False)
        send(s + 1, i)
        late = i - RELAYED
        pl.when(jnp.logical_and(late >= 0, late < RELAYED))(lambda: forward(s + 1, late))
        return carry

    for i in range(RELAYED):
        forward(0, i)
    lax.fori_loop(0, (ITERS - 1) * ny, middle, 0)

    def final(i, carry):
        advance(ITERS - 1, row_at(i), True)
        return carry

    lax.fori_loop(0, ny, final, 0)

    def sent(n, carry):
        s, i = n // ny, n % ny
        y, passed = row_at(i), jnp.logical_and(outer, i < RELAYED)
        pl.when(jnp.logical_or(above, passed))(lambda: z_up(s, y).wait_send())
        pl.when(jnp.logical_or(below, passed))(lambda: z_down(s, y).wait_send())
        return carry

    lax.fori_loop(0, ITERS * ny, sent, 0)
    for s in range(ITERS):
        pl.when(after)(lambda: y_up(s).wait_send())
        pl.when(before)(lambda: y_down(s).wait_send())


def shards(fodf, directions, signs):
    orientations, ny, nz, _ = fodf.shape
    f32, vmem, dma = jnp.float32, pltpu.VMEM, pltpu.SemaphoreType.DMA
    rows = fodf.reshape(orientations, ny * nz, 1, LANES)
    enhanced = pl.pallas_call(
        kernel,
        out_shape=vmem((orientations * ny * nz, LANES), f32),
        in_specs=[pl.BlockSpec(memory_space=pltpu.HBM)] * 3,
        out_specs=pl.BlockSpec(memory_space=vmem),
        scratch_shapes=[
            vmem((ny * nz, orientations, LANES), f32),
            vmem((3, orientations), f32),
            vmem((3, orientations), jnp.int32),
            vmem((7, HALF, LANES), f32),
            vmem((MODES_PAD, LANES), f32),
            vmem((MODES_PAD, LANES), f32),
            vmem((MODES_PAD, LANES), f32),
            vmem((MODES_PAD, LANES), f32),
            vmem((HALF, HALF), jnp.bfloat16),
            vmem((HALF, HALF), jnp.bfloat16),
            vmem((HALF, nz * LANES), f32),
            vmem((ITERS, nz + 1, ny, HALF, LANES), f32),
            vmem((ITERS, nz + 1, ny, HALF, LANES), f32),
            vmem((ITERS, nz, ny + 1, HALF, LANES), f32),
            vmem((ITERS, nz, ny + 1, HALF, LANES), f32),
            vmem((ITERS, RELAYED, HALF, LANES), f32),
            dma((ny * nz,)),
            dma((2,)),
            dma((2, ITERS, ny)),
            dma((2, ITERS, ny)),
            dma((2, ITERS)),
            dma((2, ITERS)),
            dma((ITERS, RELAYED)),
        ],
        compiler_params=pltpu.CompilerParams(
            collective_id=0, has_side_effects=True, vmem_limit_bytes=48 * 1024 * 1024
        ),
    )(*(pltpu.with_memory_space_constraint(a, pltpu.HBM) for a in (rows, directions, signs)))
    return enhanced.reshape(fodf.shape)


def solution(mesh):
    placed = (P(None, "gy", "gz", None), P(), P())
    return jax.shard_map(
        shards, mesh=mesh, in_specs=placed, out_specs=P(None, "gy", "gz", None), check_vma=False
    )
```

```python
import math

import jax
import jax.numpy as jnp
from jax import lax
from jax.experimental import pallas as pl
from jax.experimental.pallas import tpu as pltpu
from jax.sharding import PartitionSpec as P

LMAX = 8
ITERS = 4
TIME_STEP = 0.5
DIFFUSION = 0.02

HALF = 96
LANES = 128
MODES = 45
MODES_PAD = 48
CHUNK = 16
RELAYED = 3
HIGHEST = lax.Precision.HIGHEST
MESH = pl.DeviceIdType.MESH

AX, AY, AZ, CENTER, SX, SY, SZ = range(7)


def double_factorial(value):
    result = 1
    while value > 1:
        result = result * value
        value = value - 2
    return result


def harmonic_rows(along_x, along_y, along_z):
    cosines = [jnp.ones_like(along_x)]
    sines = [jnp.zeros_like(along_x)]
    for order in range(1, LMAX + 1):
        cosines.append(cosines[-1] * along_x - sines[-1] * along_y)
        sines.append(cosines[-2] * along_y + sines[-1] * along_x)
    legendre = {}
    for order in range(LMAX + 1):
        legendre[order, order] = double_factorial(2 * order - 1) * jnp.ones_like(along_z)
        if order + 1 <= LMAX:
            legendre[order + 1, order] = (2 * order + 1) * along_z * legendre[order, order]
        for degree in range(order + 2, LMAX + 1):
            legendre[degree, order] = (
                (2 * degree - 1) * along_z * legendre[degree - 1, order]
                - (degree + order - 1) * legendre[degree - 2, order]
            ) * (1.0 / (degree - order))
    rows = []
    for degree in range(0, LMAX + 1, 2):
        for order in range(degree + 1):
            norm = math.sqrt(
                (2 * degree + 1) * math.factorial(degree - order) / math.factorial(degree + order)
            )
            eigenvalue = -float(degree * (degree + 1))
            scaled = norm * legendre[degree, order]
            rows.append((scaled * cosines[order], eigenvalue))
            if order > 0:
                rows.append((scaled * sines[order], eigenvalue))
    return rows


def angular_matrix(dirs, basis, scaled, left, right):
    valid = lax.broadcasted_iota(jnp.int32, (1, LANES), 1) < HALF
    basis[...] = jnp.zeros_like(basis)
    scaled[...] = jnp.zeros_like(scaled)
    left[...] = jnp.zeros_like(left)
    right[...] = jnp.zeros_like(right)
    along = [dirs[a : a + 1, 0:LANES] for a in range(3)]
    for j, (row, eigenvalue) in enumerate(harmonic_rows(*along)):
        row = jnp.where(valid, row, 0.0)
        basis[j : j + 1, :] = row
        scaled[j : j + 1, :] = (TIME_STEP * DIFFUSION * eigenvalue) * row
    b, s = basis[...], scaled[...]
    gram = 2.0 * lax.dot_general(
        b, jnp.concatenate([b, jnp.zeros((LANES - MODES_PAD, LANES), jnp.float32)], 0),
        (((1,), (1,)), ((), ())), precision=HIGHEST, preferred_element_type=jnp.float32,
    )
    index = lax.broadcasted_iota(jnp.int32, (MODES_PAD, LANES), 0)
    for k in range(MODES):
        column = jnp.broadcast_to(gram[:, k : k + 1], (MODES_PAD, LANES))
        inverse = 1.0 / column[k : k + 1, :]
        gram_row, b_row, s_row = gram[k : k + 1, :], b[k : k + 1, :], s[k : k + 1, :]
        left[k : k + 1, :] = s_row
        right[k : k + 1, :] = b_row * inverse
        if k + 1 < MODES:
            factor = jnp.where(index > k, column, 0.0)
            gram = gram - factor * (gram_row * inverse)
            b = b - factor * (b_row * inverse)
            s = s - factor * (s_row * inverse)
    return lax.dot_general(
        left[...].T, right[...], (((1,), (0,)), ((), ())), precision=HIGHEST,
        preferred_element_type=jnp.float32,
    )


def kernel(
    fodf, dirs_hbm, signs_hbm, out,
    stage, dirs, signs, coef, basis, scaled, left, right, mat_hi, mat_lo, angular, p, q, u, v, relay,
    in_sem, small_sem, z_send, z_recv, y_send, y_recv, relay_recv,
):
    ny, nz = p.shape[2], u.shape[1]

    def row_at(i):
        return (i + ny - 1) % ny

    gz, gy = lax.axis_index("gz"), lax.axis_index("gy")
    gz_last, gy_last = lax.axis_size("gz") - 1, lax.axis_size("gy") - 1
    below, above = gz > 0, gz < gz_last
    before, after = gy > 0, gy < gy_last
    seam_high = (gz_last + 1) // 2
    seam_low = seam_high - 1
    is_low, is_high, is_first, is_last = gz == seam_low, gz == seam_high, gz == 0, gz == gz_last

    def load(r):
        return pltpu.make_async_copy(fodf.at[:, r, 0, :], stage.at[r], in_sem.at[r])

    def z_up(s, y):
        return pltpu.make_async_remote_copy(
            p.at[s, nz, y], p.at[s, 0, y], z_send.at[0, s, y], z_recv.at[0, s, y],
            device_id=(gz + 1, gy), device_id_type=MESH,
        )

    def z_down(s, y):
        return pltpu.make_async_remote_copy(
            q.at[s, 0, y], q.at[s, nz, y], z_send.at[1, s, y], z_recv.at[1, s, y],
            device_id=(gz - 1, gy), device_id_type=MESH,
        )

    def is_relayed(s, i):
        return jnp.where(s == 0, i >= ny - RELAYED, i < RELAYED)

    def relay_up(s, i):
        return pltpu.make_async_remote_copy(
            p.at[s, nz, row_at(i)], relay.at[s, i % (ny - RELAYED)], z_send.at[0, s, row_at(i)], relay_recv.at[s, i % (ny - RELAYED)],
            device_id=(0, gy), device_id_type=MESH,
        )

    def relay_down(s, i):
        return pltpu.make_async_remote_copy(
            q.at[s, 0, row_at(i)], relay.at[s, i % (ny - RELAYED)], z_send.at[1, s, row_at(i)], relay_recv.at[s, i % (ny - RELAYED)],
            device_id=(gz_last, gy), device_id_type=MESH,
        )

    def forward_up(s, i):
        return pltpu.make_async_remote_copy(
            relay.at[s, i % (ny - RELAYED)], p.at[s, 0, row_at(i)], z_send.at[1, s, row_at(i)], z_recv.at[0, s, row_at(i)],
            device_id=(seam_high, gy), device_id_type=MESH,
        )

    def forward_down(s, i):
        return pltpu.make_async_remote_copy(
            relay.at[s, i % (ny - RELAYED)], q.at[s, nz, row_at(i)], z_send.at[0, s, row_at(i)], z_recv.at[1, s, row_at(i)],
            device_id=(seam_low, gy), device_id_type=MESH,
        )

    def y_up(s):
        return pltpu.make_async_remote_copy(
            u.at[s, :, ny], u.at[s, :, 0], y_send.at[0, s], y_recv.at[0, s],
            device_id=(gz, gy + 1), device_id_type=MESH,
        )

    def y_down(s):
        return pltpu.make_async_remote_copy(
            v.at[s, :, 0], v.at[s, :, ny], y_send.at[1, s], y_recv.at[1, s],
            device_id=(gz, gy - 1), device_id_type=MESH,
        )

    def send(s, i):
        y, far = row_at(i), is_relayed(s, i)
        round_up, round_down = jnp.logical_and(is_low, far), jnp.logical_and(is_high, far)
        pl.when(jnp.logical_and(above, jnp.logical_not(round_up)))(lambda: z_up(s, y).start())
        pl.when(jnp.logical_and(below, jnp.logical_not(round_down)))(lambda: z_down(s, y).start())
        pl.when(round_up)(lambda: relay_up(s, i).start())
        pl.when(round_down)(lambda: relay_down(s, i).start())
        pl.when(jnp.logical_and(y == 0, before))(lambda: y_down(s).start())
        pl.when(jnp.logical_and(y == ny - 1, after))(lambda: y_up(s).start())

    def receive(s, y):
        pl.when(below)(lambda: z_up(s, y).wait_recv())
        pl.when(above)(lambda: z_down(s, y).wait_recv())
        pl.when(jnp.logical_and(y == 0, before))(lambda: y_up(s).wait_recv())
        pl.when(jnp.logical_and(y == ny - 1, after))(lambda: y_down(s).wait_recv())

    def forward(s, i):
        @pl.when(is_first)
        def _():
            relay_up(s, i).wait_recv()
            forward_up(s, i).start()

        @pl.when(is_last)
        def _():
            relay_down(s, i).wait_recv()
            forward_down(s, i).start()

    small = [
        pltpu.make_async_copy(dirs_hbm, dirs, small_sem.at[0]),
        pltpu.make_async_copy(signs_hbm, signs, small_sem.at[1]),
    ]
    for copy in small:
        copy.start()
    for i in range(ny):
        for z in range(nz):
            load(row_at(i) * nz + z).start()

    barrier = pltpu.get_barrier_semaphore()
    inner, outer = jnp.logical_or(is_low, is_high), jnp.logical_or(is_first, is_last)
    greeted = [(below, (gz - 1, gy)), (above, (gz + 1, gy)), (before, (gz, gy - 1)), (after, (gz, gy + 1))]
    greeted += [(inner, (0, gy)), (inner, (gz_last, gy)), (outer, (seam_low, gy)), (outer, (seam_high, gy))]
    for there, target in greeted:
        @pl.when(there)
        def _():
            pl.semaphore_signal(barrier, inc=1, device_id=target, device_id_type=MESH)

    @pl.when(gz == 0)
    def _():
        p[:, 0] = jnp.zeros_like(p[:, 0])

    @pl.when(gz == gz_last)
    def _():
        q[:, nz] = jnp.zeros_like(q[:, nz])

    @pl.when(gy == 0)
    def _():
        u[:, :, 0] = jnp.zeros_like(u[:, :, 0])

    @pl.when(gy == gy_last)
    def _():
        v[:, :, ny] = jnp.zeros_like(v[:, :, ny])

    for copy in small:
        copy.wait()
    half_speed = TIME_STEP * jnp.abs(dirs[:, 0:LANES])
    sign = signs[:, 0:LANES].astype(jnp.float32)
    sign_z = sign[2:3]
    rows = [half_speed[0:1], half_speed[1:2], half_speed[2:3]]
    rows.append(1.0 - (rows[0] + rows[1] + rows[2]))
    rows += [sign[0:1] * sign_z, sign[1:2] * sign_z, sign_z]
    table = jnp.concatenate(rows + [jnp.zeros((LANES - len(rows), LANES), jnp.float32)], 0).T

    def spread(c):
        coef[c] = jnp.broadcast_to(table[0:HALF, c : c + 1], (HALF, LANES))

    spread(SZ)
    spread(SY)

    peers = sum(there.astype(jnp.int32) for there, _ in greeted)
    pl.semaphore_wait(barrier, peers)

    def first(i, carry):
        y = row_at(i)
        for z in range(nz):
            r = y * nz + z
            load(r).wait()
            for c in range(0, HALF, CHUNK):
                lines = slice(c, c + CHUNK)
                one, other = stage[r, c : c + CHUNK, :], stage[r, HALF + c : HALF + c + CHUNK, :]
                upward, along_y = coef[SZ, lines] > 0, coef[SY, lines] > 0
                up, down = jnp.where(upward, one, other), jnp.where(upward, other, one)
                p[0, z + 1, y, lines] = up
                q[0, z, y, lines] = down
                u[0, z, y + 1, lines] = jnp.where(along_y, up, down)
                v[0, z, y, lines] = jnp.where(along_y, down, up)
        send(0, i)
        return carry

    lax.fori_loop(0, ny, first, 0)
    for c in (AX, AY, AZ, CENTER, SX):
        spread(c)

    matrix = angular_matrix(dirs, basis, scaled, left, right)[0:HALF, 0:HALF]
    high = matrix.astype(jnp.bfloat16)
    mat_hi[...] = high
    mat_lo[...] = (matrix - high.astype(jnp.float32)).astype(jnp.bfloat16)

    lane = lax.broadcasted_iota(jnp.int32, (CHUNK, LANES), 1)

    def advance(s, y, last):
        total = jnp.concatenate([p[s, z + 1, y] + q[s, z, y] for z in range(nz)], 1)
        total_hi = total.astype(jnp.bfloat16)
        total_lo = (total - total_hi.astype(jnp.float32)).astype(jnp.bfloat16)
        hi, lo = mat_hi[...], mat_lo[...]
        angular[...] = (
            jnp.dot(hi, total_hi, preferred_element_type=jnp.float32)
            + jnp.dot(hi, total_lo, preferred_element_type=jnp.float32)
            + jnp.dot(lo, total_hi, preferred_element_type=jnp.float32)
        )
        receive(s, y)
        for z in range(nz):
            for c in range(0, HALF, CHUNK):
                lines = slice(c, c + CHUNK)
                up, down = p[s, z + 1, y, lines], q[s, z, y, lines]
                along_x, along_y = coef[SX, lines] > 0, coef[SY, lines] > 0
                rising, falling = jnp.where(along_x, up, down), jnp.where(along_x, down, up)
                rising = jnp.where(lane == 0, 0.0, pltpu.roll(rising, 1, 1))
                falling = jnp.where(lane == LANES - 1, 0.0, pltpu.roll(falling, LANES - 1, 1))
                y_low, y_high = u[s, z, y, lines], v[s, z, y + 1, lines]
                ang = angular[lines, z * LANES : (z + 1) * LANES]
                ax, ay, az, center = (coef[i, lines] for i in (AX, AY, AZ, CENTER))
                new_up = (
                    center * up + ang + ax * jnp.where(along_x, rising, falling)
                    + ay * jnp.where(along_y, y_low, y_high) + az * p[s, z, y, lines]
                )
                new_down = (
                    center * down + ang + ax * jnp.where(along_x, falling, rising)
                    + ay * jnp.where(along_y, y_high, y_low) + az * q[s, z + 1, y, lines]
                )
                if last:
                    r = y * nz + z
                    upward = coef[SZ, lines] > 0
                    one, other = jnp.where(upward, new_up, new_down), jnp.where(upward, new_down, new_up)
                    out[pl.ds(c * ny * nz + r, CHUNK, stride=ny * nz), :] = one
                    out[pl.ds((HALF + c) * ny * nz + r, CHUNK, stride=ny * nz), :] = other
                else:
                    p[s + 1, z + 1, y, lines] = new_up
                    q[s + 1, z, y, lines] = new_down
                    u[s + 1, z, y + 1, lines] = jnp.where(along_y, new_up, new_down)
                    v[s + 1, z, y, lines] = jnp.where(along_y, new_down, new_up)

    def middle(n, carry):
        s, i = n // ny, n % ny
        advance(s, row_at(i), False)
        send(s + 1, i)
        late = i - 4
        pl.when(jnp.logical_and(late >= 0, late < RELAYED))(lambda: forward(s + 1, late))
        return carry

    for i in range(ny - RELAYED, ny):
        forward(0, i)
    lax.fori_loop(0, (ITERS - 1) * ny, middle, 0)

    def sent(s, i):
        y, passed = row_at(i), jnp.logical_and(outer, is_relayed(s, i))
        pl.when(jnp.logical_or(above, passed))(lambda: z_up(s, y).wait_send())
        pl.when(jnp.logical_or(below, passed))(lambda: z_down(s, y).wait_send())

    def y_sent(s):
        pl.when(after)(lambda: y_up(s).wait_send())
        pl.when(before)(lambda: y_down(s).wait_send())

    def final(i, carry):
        for s in range(ITERS - 1):
            sent(s, i)
        advance(ITERS - 1, row_at(i), True)
        return carry

    for s in range(ITERS - 1):
        y_sent(s)
    lax.fori_loop(0, ny, final, 0)
    for i in range(ny):
        sent(ITERS - 1, i)
    y_sent(ITERS - 1)


def shards(fodf, directions, signs):
    orientations, ny, nz, _ = fodf.shape
    f32, vmem, dma = jnp.float32, pltpu.VMEM, pltpu.SemaphoreType.DMA
    rows = fodf.reshape(orientations, ny * nz, 1, LANES)
    enhanced = pl.pallas_call(
        kernel,
        out_shape=vmem((orientations * ny * nz, LANES), f32),
        in_specs=[pl.BlockSpec(memory_space=pltpu.HBM)] * 3,
        out_specs=pl.BlockSpec(memory_space=vmem),
        scratch_shapes=[
            vmem((ny * nz, orientations, LANES), f32),
            vmem((3, orientations), f32),
            vmem((3, orientations), jnp.int32),
            vmem((7, HALF, LANES), f32),
            vmem((MODES_PAD, LANES), f32),
            vmem((MODES_PAD, LANES), f32),
            vmem((MODES_PAD, LANES), f32),
            vmem((MODES_PAD, LANES), f32),
            vmem((HALF, HALF), jnp.bfloat16),
            vmem((HALF, HALF), jnp.bfloat16),
            vmem((HALF, nz * LANES), f32),
            vmem((ITERS, nz + 1, ny, HALF, LANES), f32),
            vmem((ITERS, nz + 1, ny, HALF, LANES), f32),
            vmem((ITERS, nz, ny + 1, HALF, LANES), f32),
            vmem((ITERS, nz, ny + 1, HALF, LANES), f32),
            vmem((ITERS, RELAYED, HALF, LANES), f32),
            dma((ny * nz,)),
            dma((2,)),
            dma((2, ITERS, ny)),
            dma((2, ITERS, ny)),
            dma((2, ITERS)),
            dma((2, ITERS)),
            dma((ITERS, RELAYED)),
        ],
        compiler_params=pltpu.CompilerParams(
            collective_id=0, has_side_effects=True, vmem_limit_bytes=48 * 1024 * 1024
        ),
    )(*(pltpu.with_memory_space_constraint(a, pltpu.HBM) for a in (rows, directions, signs)))
    return enhanced.reshape(fodf.shape)


def solution(mesh):
    placed = (P(None, "gy", "gz", None), P(), P())
    return jax.shard_map(
        shards, mesh=mesh, in_specs=placed, out_specs=P(None, "gy", "gz", None), check_vma=False
    )
```

```python
import math

import jax
import jax.numpy as jnp
from jax import lax
from jax.experimental import pallas as pl
from jax.experimental.pallas import tpu as pltpu
from jax.sharding import PartitionSpec as P

LMAX = 8
ITERS = 4
TIME_STEP = 0.5
DIFFUSION = 0.02

HALF = 96
LANES = 128
MODES = 45
MODES_PAD = 48
CHUNK = 16
LAG = 4
RELAYED = 4
HIGHEST = lax.Precision.HIGHEST
MESH = pl.DeviceIdType.MESH

AX, AY, AZ, CENTER, SX, SY, SZ = range(7)


def double_factorial(value):
    result = 1
    while value > 1:
        result = result * value
        value = value - 2
    return result


def harmonic_rows(along_x, along_y, along_z):
    cosines = [jnp.ones_like(along_x)]
    sines = [jnp.zeros_like(along_x)]
    for order in range(1, LMAX + 1):
        cosines.append(cosines[-1] * along_x - sines[-1] * along_y)
        sines.append(cosines[-2] * along_y + sines[-1] * along_x)
    legendre = {}
    for order in range(LMAX + 1):
        legendre[order, order] = double_factorial(2 * order - 1) * jnp.ones_like(along_z)
        if order + 1 <= LMAX:
            legendre[order + 1, order] = (2 * order + 1) * along_z * legendre[order, order]
        for degree in range(order + 2, LMAX + 1):
            legendre[degree, order] = (
                (2 * degree - 1) * along_z * legendre[degree - 1, order]
                - (degree + order - 1) * legendre[degree - 2, order]
            ) * (1.0 / (degree - order))
    rows = []
    for degree in range(0, LMAX + 1, 2):
        for order in range(degree + 1):
            norm = math.sqrt(
                (2 * degree + 1) * math.factorial(degree - order) / math.factorial(degree + order)
            )
            eigenvalue = -float(degree * (degree + 1))
            scaled = norm * legendre[degree, order]
            rows.append((scaled * cosines[order], eigenvalue))
            if order > 0:
                rows.append((scaled * sines[order], eigenvalue))
    return rows


def angular_matrix(dirs, basis, scaled, left, right):
    valid = lax.broadcasted_iota(jnp.int32, (1, LANES), 1) < HALF
    basis[...] = jnp.zeros_like(basis)
    scaled[...] = jnp.zeros_like(scaled)
    left[...] = jnp.zeros_like(left)
    right[...] = jnp.zeros_like(right)
    along = [dirs[a : a + 1, 0:LANES] for a in range(3)]
    for j, (row, eigenvalue) in enumerate(harmonic_rows(*along)):
        row = jnp.where(valid, row, 0.0)
        basis[j : j + 1, :] = row
        scaled[j : j + 1, :] = (TIME_STEP * DIFFUSION * eigenvalue) * row
    b, s = basis[...], scaled[...]
    gram = 2.0 * lax.dot_general(
        b, jnp.concatenate([b, jnp.zeros((LANES - MODES_PAD, LANES), jnp.float32)], 0),
        (((1,), (1,)), ((), ())), precision=HIGHEST, preferred_element_type=jnp.float32,
    )
    index = lax.broadcasted_iota(jnp.int32, (MODES_PAD, LANES), 0)
    for k in range(MODES):
        column = jnp.broadcast_to(gram[:, k : k + 1], (MODES_PAD, LANES))
        inverse = 1.0 / column[k : k + 1, :]
        gram_row, b_row, s_row = gram[k : k + 1, :], b[k : k + 1, :], s[k : k + 1, :]
        left[k : k + 1, :] = s_row
        right[k : k + 1, :] = b_row * inverse
        if k + 1 < MODES:
            factor = jnp.where(index > k, column, 0.0)
            gram = gram - factor * (gram_row * inverse)
            b = b - factor * (b_row * inverse)
            s = s - factor * (s_row * inverse)
    return lax.dot_general(
        left[...].T, right[...], (((1,), (0,)), ((), ())), precision=HIGHEST,
        preferred_element_type=jnp.float32,
    )


def kernel(
    fodf, dirs_hbm, signs_hbm, out,
    stage, dirs, signs, coef, basis, scaled, left, right, mat_hi, mat_lo, angular, p, q, u, v, relay,
    in_sem, small_sem, z_send, z_recv, y_send, y_recv, relay_recv,
):
    ny, nz = p.shape[2], u.shape[1]

    def row_at(i):
        return (i + ny - 1) % ny

    gz, gy = lax.axis_index("gz"), lax.axis_index("gy")
    gz_last, gy_last = lax.axis_size("gz") - 1, lax.axis_size("gy") - 1
    below, above = gz > 0, gz < gz_last
    before, after = gy > 0, gy < gy_last
    seam_high = (gz_last + 1) // 2
    seam_low = seam_high - 1
    is_low, is_high, is_first, is_last = gz == seam_low, gz == seam_high, gz == 0, gz == gz_last

    def load(r):
        return pltpu.make_async_copy(fodf.at[:, r, 0, :], stage.at[r], in_sem.at[r])

    def z_up(s, y):
        return pltpu.make_async_remote_copy(
            p.at[s, nz, y], p.at[s, 0, y], z_send.at[0, s, y], z_recv.at[0, s, y],
            device_id=(gz + 1, gy), device_id_type=MESH,
        )

    def z_down(s, y):
        return pltpu.make_async_remote_copy(
            q.at[s, 0, y], q.at[s, nz, y], z_send.at[1, s, y], z_recv.at[1, s, y],
            device_id=(gz - 1, gy), device_id_type=MESH,
        )

    def relay_up(s, i):
        return pltpu.make_async_remote_copy(
            p.at[s, nz, row_at(i)], relay.at[s, i], z_send.at[0, s, row_at(i)], relay_recv.at[s, i],
            device_id=(0, gy), device_id_type=MESH,
        )

    def relay_down(s, i):
        return pltpu.make_async_remote_copy(
            q.at[s, 0, row_at(i)], relay.at[s, i], z_send.at[1, s, row_at(i)], relay_recv.at[s, i],
            device_id=(gz_last, gy), device_id_type=MESH,
        )

    def forward_up(s, i):
        return pltpu.make_async_remote_copy(
            relay.at[s, i], p.at[s, 0, row_at(i)], z_send.at[1, s, row_at(i)], z_recv.at[0, s, row_at(i)],
            device_id=(seam_high, gy), device_id_type=MESH,
        )

    def forward_down(s, i):
        return pltpu.make_async_remote_copy(
            relay.at[s, i], q.at[s, nz, row_at(i)], z_send.at[0, s, row_at(i)], z_recv.at[1, s, row_at(i)],
            device_id=(seam_low, gy), device_id_type=MESH,
        )

    def y_up(s):
        return pltpu.make_async_remote_copy(
            u.at[s, :, ny], u.at[s, :, 0], y_send.at[0, s], y_recv.at[0, s],
            device_id=(gz, gy + 1), device_id_type=MESH,
        )

    def y_down(s):
        return pltpu.make_async_remote_copy(
            v.at[s, :, 0], v.at[s, :, ny], y_send.at[1, s], y_recv.at[1, s],
            device_id=(gz, gy - 1), device_id_type=MESH,
        )

    def send_z(s, i):
        y, far = row_at(i), i < RELAYED
        round_up, round_down = jnp.logical_and(is_low, far), jnp.logical_and(is_high, far)
        pl.when(jnp.logical_and(above, jnp.logical_not(round_up)))(lambda: z_up(s, y).start())
        pl.when(jnp.logical_and(below, jnp.logical_not(round_down)))(lambda: z_down(s, y).start())
        pl.when(round_up)(lambda: relay_up(s, i).start())
        pl.when(round_down)(lambda: relay_down(s, i).start())

    def send_y(s, y):
        pl.when(jnp.logical_and(y == 0, before))(lambda: y_down(s).start())
        pl.when(jnp.logical_and(y == ny - 1, after))(lambda: y_up(s).start())

    def receive_z(s, y):
        pl.when(below)(lambda: z_up(s, y).wait_recv())
        pl.when(above)(lambda: z_down(s, y).wait_recv())

    def receive_y(s, y):
        pl.when(jnp.logical_and(y == 0, before))(lambda: y_up(s).wait_recv())
        pl.when(jnp.logical_and(y == ny - 1, after))(lambda: y_down(s).wait_recv())

    def forward(s, i):
        @pl.when(is_first)
        def _():
            relay_up(s, i).wait_recv()
            forward_up(s, i).start()

        @pl.when(is_last)
        def _():
            relay_down(s, i).wait_recv()
            forward_down(s, i).start()

    small = [
        pltpu.make_async_copy(dirs_hbm, dirs, small_sem.at[0]),
        pltpu.make_async_copy(signs_hbm, signs, small_sem.at[1]),
    ]
    for copy in small:
        copy.start()
    for i in range(ny):
        for z in range(nz):
            load(row_at(i) * nz + z).start()

    barrier = pltpu.get_barrier_semaphore()
    inner, outer = jnp.logical_or(is_low, is_high), jnp.logical_or(is_first, is_last)
    greeted = [(below, (gz - 1, gy)), (above, (gz + 1, gy)), (before, (gz, gy - 1)), (after, (gz, gy + 1))]
    greeted += [(inner, (0, gy)), (inner, (gz_last, gy)), (outer, (seam_low, gy)), (outer, (seam_high, gy))]
    for there, target in greeted:
        @pl.when(there)
        def _():
            pl.semaphore_signal(barrier, inc=1, device_id=target, device_id_type=MESH)

    @pl.when(gz == 0)
    def _():
        p[0:ITERS, 0] = jnp.zeros_like(p[0:ITERS, 0])

    @pl.when(gz == gz_last)
    def _():
        q[0:ITERS, nz] = jnp.zeros_like(q[0:ITERS, nz])

    @pl.when(gy == 0)
    def _():
        u[:, :, 0] = jnp.zeros_like(u[:, :, 0])

    @pl.when(gy == gy_last)
    def _():
        v[:, :, ny] = jnp.zeros_like(v[:, :, ny])

    for copy in small:
        copy.wait()
    half_speed = TIME_STEP * jnp.abs(dirs[:, 0:LANES])
    sign = signs[:, 0:LANES].astype(jnp.float32)
    sign_z = sign[2:3]
    rows = [half_speed[0:1], half_speed[1:2], half_speed[2:3]]
    rows.append(1.0 - (rows[0] + rows[1] + rows[2]))
    rows += [sign[0:1] * sign_z, sign[1:2] * sign_z, sign_z]
    table = jnp.concatenate(rows + [jnp.zeros((LANES - len(rows), LANES), jnp.float32)], 0).T

    def spread(c):
        coef[c] = jnp.broadcast_to(table[0:HALF, c : c + 1], (HALF, LANES))

    spread(SZ)
    spread(SY)

    peers = sum(there.astype(jnp.int32) for there, _ in greeted)
    pl.semaphore_wait(barrier, peers)

    def first(i, carry):
        y = row_at(i)
        for z in range(nz):
            r = y * nz + z
            load(r).wait()
            for c in range(0, HALF, CHUNK):
                lines = slice(c, c + CHUNK)
                one, other = stage[r, c : c + CHUNK, :], stage[r, HALF + c : HALF + c + CHUNK, :]
                upward, along_y = coef[SZ, lines] > 0, coef[SY, lines] > 0
                up, down = jnp.where(upward, one, other), jnp.where(upward, other, one)
                p[0, z + 1, y, lines] = up
                q[0, z, y, lines] = down
                u[0, z, y + 1, lines] = jnp.where(along_y, up, down)
                v[0, z, y, lines] = jnp.where(along_y, down, up)
        send_z(0, i)
        send_y(0, y)
        return carry

    lax.fori_loop(0, ny, first, 0)
    for c in (AX, AY, AZ, CENTER, SX):
        spread(c)

    matrix = angular_matrix(dirs, basis, scaled, left, right)[0:HALF, 0:HALF]
    high = matrix.astype(jnp.bfloat16)
    mat_hi[...] = high
    mat_lo[...] = (matrix - high.astype(jnp.float32)).astype(jnp.bfloat16)

    lane = lax.broadcasted_iota(jnp.int32, (CHUNK, LANES), 1)

    def local(s, y):
        receive_y(s, y)
        total = jnp.concatenate([p[s, z + 1, y] + q[s, z, y] for z in range(nz)], 1)
        total_hi = total.astype(jnp.bfloat16)
        total_lo = (total - total_hi.astype(jnp.float32)).astype(jnp.bfloat16)
        hi, lo = mat_hi[...], mat_lo[...]
        angular[...] = (
            jnp.dot(hi, total_hi, preferred_element_type=jnp.float32)
            + jnp.dot(hi, total_lo, preferred_element_type=jnp.float32)
            + jnp.dot(lo, total_hi, preferred_element_type=jnp.float32)
        )
        for z in range(nz):
            for c in range(0, HALF, CHUNK):
                lines = slice(c, c + CHUNK)
                up, down = p[s, z + 1, y, lines], q[s, z, y, lines]
                along_x, along_y = coef[SX, lines] > 0, coef[SY, lines] > 0
                rising, falling = jnp.where(along_x, up, down), jnp.where(along_x, down, up)
                rising = jnp.where(lane == 0, 0.0, pltpu.roll(rising, 1, 1))
                falling = jnp.where(lane == LANES - 1, 0.0, pltpu.roll(falling, LANES - 1, 1))
                y_low, y_high = u[s, z, y, lines], v[s, z, y + 1, lines]
                ang = angular[lines, z * LANES : (z + 1) * LANES]
                ax, ay, az, center = (coef[i, lines] for i in (AX, AY, AZ, CENTER))
                new_up = (
                    center * up + ang + ax * jnp.where(along_x, rising, falling)
                    + ay * jnp.where(along_y, y_low, y_high)
                )
                new_down = (
                    center * down + ang + ax * jnp.where(along_x, falling, rising)
                    + ay * jnp.where(along_y, y_high, y_low)
                )
                if z > 0:
                    new_up += az * p[s, z, y, lines]
                if z < nz - 1:
                    new_down += az * q[s, z + 1, y, lines]
                p[s + 1, z + 1, y, lines] = new_up
                q[s + 1, z, y, lines] = new_down

    def finish(s, y, last):
        receive_z(s, y)
        for c in range(0, HALF, CHUNK):
            lines = slice(c, c + CHUNK)
            az = coef[AZ, lines]
            for z in range(nz):
                up, down = p[s + 1, z + 1, y, lines], q[s + 1, z, y, lines]
                if z == 0:
                    up += az * p[s, 0, y, lines]
                if z == nz - 1:
                    down += az * q[s, nz, y, lines]
                if last:
                    r = y * nz + z
                    upward = coef[SZ, lines] > 0
                    one, other = jnp.where(upward, up, down), jnp.where(upward, down, up)
                    out[pl.ds(c * ny * nz + r, CHUNK, stride=ny * nz), :] = one
                    out[pl.ds((HALF + c) * ny * nz + r, CHUNK, stride=ny * nz), :] = other
                else:
                    along_y = coef[SY, lines] > 0
                    if z == 0:
                        p[s + 1, 1, y, lines] = up
                    if z == nz - 1:
                        q[s + 1, nz - 1, y, lines] = down
                    u[s + 1, z, y + 1, lines] = jnp.where(along_y, up, down)
                    v[s + 1, z, y, lines] = jnp.where(along_y, down, up)

    def sent(s, i):
        y, passed = row_at(i), jnp.logical_and(outer, i < RELAYED)
        pl.when(jnp.logical_or(above, passed))(lambda: z_up(s, y).wait_send())
        pl.when(jnp.logical_or(below, passed))(lambda: z_down(s, y).wait_send())

    def y_sent(s):
        pl.when(after)(lambda: y_up(s).wait_send())
        pl.when(before)(lambda: y_down(s).wait_send())

    for i in range(RELAYED):
        forward(0, i)

    def step(s, carry):
        def ahead(i, carry):
            local(s, row_at(i))
            send_z(s + 1, i)
            return carry

        def behind(i, carry):
            finish(s, row_at(i), False)
            send_y(s + 1, row_at(i))
            late = i - LAG
            pl.when(jnp.logical_and(late >= 0, late < RELAYED))(lambda: forward(s + 1, late))
            return carry

        lax.fori_loop(0, ny, ahead, 0)
        lax.fori_loop(0, ny, behind, 0)
        return carry

    lax.fori_loop(0, ITERS - 1, step, 0)

    def ahead(i, carry):
        for s in range(ITERS - 1):
            sent(s, i)
        local(ITERS - 1, row_at(i))
        return carry

    def behind(i, carry):
        finish(ITERS - 1, row_at(i), True)
        return carry

    lax.fori_loop(0, ny, ahead, 0)
    for s in range(ITERS):
        y_sent(s)
    lax.fori_loop(0, ny, behind, 0)
    for i in range(ny):
        sent(ITERS - 1, i)


def shards(fodf, directions, signs):
    orientations, ny, nz, _ = fodf.shape
    f32, vmem, dma = jnp.float32, pltpu.VMEM, pltpu.SemaphoreType.DMA
    rows = fodf.reshape(orientations, ny * nz, 1, LANES)
    enhanced = pl.pallas_call(
        kernel,
        out_shape=vmem((orientations * ny * nz, LANES), f32),
        in_specs=[pl.BlockSpec(memory_space=pltpu.HBM)] * 3,
        out_specs=pl.BlockSpec(memory_space=vmem),
        scratch_shapes=[
            vmem((ny * nz, orientations, LANES), f32),
            vmem((3, orientations), f32),
            vmem((3, orientations), jnp.int32),
            vmem((7, HALF, LANES), f32),
            vmem((MODES_PAD, LANES), f32),
            vmem((MODES_PAD, LANES), f32),
            vmem((MODES_PAD, LANES), f32),
            vmem((MODES_PAD, LANES), f32),
            vmem((HALF, HALF), jnp.bfloat16),
            vmem((HALF, HALF), jnp.bfloat16),
            vmem((HALF, nz * LANES), f32),
            vmem((ITERS + 1, nz + 1, ny, HALF, LANES), f32),
            vmem((ITERS + 1, nz + 1, ny, HALF, LANES), f32),
            vmem((ITERS, nz, ny + 1, HALF, LANES), f32),
            vmem((ITERS, nz, ny + 1, HALF, LANES), f32),
            vmem((ITERS, RELAYED, HALF, LANES), f32),
            dma((ny * nz,)),
            dma((2,)),
            dma((2, ITERS, ny)),
            dma((2, ITERS, ny)),
            dma((2, ITERS)),
            dma((2, ITERS)),
            dma((ITERS, RELAYED)),
        ],
        compiler_params=pltpu.CompilerParams(
            collective_id=0, has_side_effects=True, vmem_limit_bytes=48 * 1024 * 1024
        ),
    )(*(pltpu.with_memory_space_constraint(a, pltpu.HBM) for a in (rows, directions, signs)))
    return enhanced.reshape(fodf.shape)


def solution(mesh):
    placed = (P(None, "gy", "gz", None), P(), P())
    return jax.shard_map(
        shards, mesh=mesh, in_specs=placed, out_specs=P(None, "gy", "gz", None), check_vma=False
    )
```

```python
import math

import jax
import jax.numpy as jnp
from jax import lax
from jax.experimental import pallas as pl
from jax.experimental.pallas import tpu as pltpu
from jax.sharding import PartitionSpec as P

LMAX = 8
ITERS = 4
TIME_STEP = 0.5
DIFFUSION = 0.02

HALF = 96
LANES = 128
MODES = 45
MODES_PAD = 48
CHUNK = 16
ROWS = 2
RELAYED = 2
HIGHEST = lax.Precision.HIGHEST
MESH = pl.DeviceIdType.MESH

AX, AY, AZ, CENTER, SX, SY, SZ = range(7)


def double_factorial(value):
    result = 1
    while value > 1:
        result = result * value
        value = value - 2
    return result


def harmonic_rows(along_x, along_y, along_z):
    cosines = [jnp.ones_like(along_x)]
    sines = [jnp.zeros_like(along_x)]
    for order in range(1, LMAX + 1):
        cosines.append(cosines[-1] * along_x - sines[-1] * along_y)
        sines.append(cosines[-2] * along_y + sines[-1] * along_x)
    legendre = {}
    for order in range(LMAX + 1):
        legendre[order, order] = double_factorial(2 * order - 1) * jnp.ones_like(along_z)
        if order + 1 <= LMAX:
            legendre[order + 1, order] = (2 * order + 1) * along_z * legendre[order, order]
        for degree in range(order + 2, LMAX + 1):
            legendre[degree, order] = (
                (2 * degree - 1) * along_z * legendre[degree - 1, order]
                - (degree + order - 1) * legendre[degree - 2, order]
            ) * (1.0 / (degree - order))
    rows = []
    for degree in range(0, LMAX + 1, 2):
        for order in range(degree + 1):
            norm = math.sqrt(
                (2 * degree + 1) * math.factorial(degree - order) / math.factorial(degree + order)
            )
            eigenvalue = -float(degree * (degree + 1))
            scaled = norm * legendre[degree, order]
            rows.append((scaled * cosines[order], eigenvalue))
            if order > 0:
                rows.append((scaled * sines[order], eigenvalue))
    return rows


def angular_matrix(dirs, basis, scaled, left, right):
    valid = lax.broadcasted_iota(jnp.int32, (1, LANES), 1) < HALF
    basis[...] = jnp.zeros_like(basis)
    scaled[...] = jnp.zeros_like(scaled)
    left[...] = jnp.zeros_like(left)
    right[...] = jnp.zeros_like(right)
    along = [dirs[a : a + 1, 0:LANES] for a in range(3)]
    for j, (row, eigenvalue) in enumerate(harmonic_rows(*along)):
        row = jnp.where(valid, row, 0.0)
        basis[j : j + 1, :] = row
        scaled[j : j + 1, :] = (TIME_STEP * DIFFUSION * eigenvalue) * row
    b, s = basis[...], scaled[...]
    gram = 2.0 * lax.dot_general(
        b, jnp.concatenate([b, jnp.zeros((LANES - MODES_PAD, LANES), jnp.float32)], 0),
        (((1,), (1,)), ((), ())), precision=HIGHEST, preferred_element_type=jnp.float32,
    )
    index = lax.broadcasted_iota(jnp.int32, (MODES_PAD, LANES), 0)
    for k in range(MODES):
        column = jnp.broadcast_to(gram[:, k : k + 1], (MODES_PAD, LANES))
        inverse = 1.0 / column[k : k + 1, :]
        gram_row, b_row, s_row = gram[k : k + 1, :], b[k : k + 1, :], s[k : k + 1, :]
        left[k : k + 1, :] = s_row
        right[k : k + 1, :] = b_row * inverse
        if k + 1 < MODES:
            factor = jnp.where(index > k, column, 0.0)
            gram = gram - factor * (gram_row * inverse)
            b = b - factor * (b_row * inverse)
            s = s - factor * (s_row * inverse)
    return lax.dot_general(
        left[...].T, right[...], (((1,), (0,)), ((), ())), precision=HIGHEST,
        preferred_element_type=jnp.float32,
    )


def kernel(
    fodf, dirs_hbm, signs_hbm, out,
    stage, dirs, signs, coef, basis, scaled, left, right, mat_hi, mat_lo, angular, p, q, u, v, relay,
    in_sem, small_sem, z_send, z_recv, y_send, y_recv, relay_recv,
):
    ny, nz = p.shape[2], u.shape[1]

    blocks = ny // ROWS
    gz, gy = lax.axis_index("gz"), lax.axis_index("gy")
    gz_last, gy_last = lax.axis_size("gz") - 1, lax.axis_size("gy") - 1
    below, above = gz > 0, gz < gz_last
    before, after = gy > 0, gy < gy_last
    seam_high = (gz_last + 1) // 2
    seam_low = seam_high - 1
    is_low, is_high, is_first, is_last = gz == seam_low, gz == seam_high, gz == 0, gz == gz_last

    def load(r):
        return pltpu.make_async_copy(fodf.at[:, r, 0, :], stage.at[r], in_sem.at[r])

    def z_up(s, i):
        return pltpu.make_async_remote_copy(
            p.at[s, nz, pl.ds(i * ROWS, ROWS)], p.at[s, 0, pl.ds(i * ROWS, ROWS)], z_send.at[0, s, i], z_recv.at[0, s, i],
            device_id=(gz + 1, gy), device_id_type=MESH,
        )

    def z_down(s, i):
        return pltpu.make_async_remote_copy(
            q.at[s, 0, pl.ds(i * ROWS, ROWS)], q.at[s, nz, pl.ds(i * ROWS, ROWS)], z_send.at[1, s, i], z_recv.at[1, s, i],
            device_id=(gz - 1, gy), device_id_type=MESH,
        )

    def relay_up(s, i):
        return pltpu.make_async_remote_copy(
            p.at[s, nz, pl.ds(i * ROWS, ROWS)], relay.at[s, i], z_send.at[0, s, i], relay_recv.at[s, i],
            device_id=(0, gy), device_id_type=MESH,
        )

    def relay_down(s, i):
        return pltpu.make_async_remote_copy(
            q.at[s, 0, pl.ds(i * ROWS, ROWS)], relay.at[s, i], z_send.at[1, s, i], relay_recv.at[s, i],
            device_id=(gz_last, gy), device_id_type=MESH,
        )

    def forward_up(s, i):
        return pltpu.make_async_remote_copy(
            relay.at[s, i], p.at[s, 0, pl.ds(i * ROWS, ROWS)], z_send.at[1, s, i], z_recv.at[0, s, i],
            device_id=(seam_high, gy), device_id_type=MESH,
        )

    def forward_down(s, i):
        return pltpu.make_async_remote_copy(
            relay.at[s, i], q.at[s, nz, pl.ds(i * ROWS, ROWS)], z_send.at[0, s, i], z_recv.at[1, s, i],
            device_id=(seam_low, gy), device_id_type=MESH,
        )

    def y_up(s):
        return pltpu.make_async_remote_copy(
            u.at[s, :, ny], u.at[s, :, 0], y_send.at[0, s], y_recv.at[0, s],
            device_id=(gz, gy + 1), device_id_type=MESH,
        )

    def y_down(s):
        return pltpu.make_async_remote_copy(
            v.at[s, :, 0], v.at[s, :, ny], y_send.at[1, s], y_recv.at[1, s],
            device_id=(gz, gy - 1), device_id_type=MESH,
        )

    def send_z(s, i):
        far = i < RELAYED
        round_up, round_down = jnp.logical_and(is_low, far), jnp.logical_and(is_high, far)
        pl.when(jnp.logical_and(above, jnp.logical_not(round_up)))(lambda: z_up(s, i).start())
        pl.when(jnp.logical_and(below, jnp.logical_not(round_down)))(lambda: z_down(s, i).start())
        pl.when(round_up)(lambda: relay_up(s, i).start())
        pl.when(round_down)(lambda: relay_down(s, i).start())

    def send_y(s, y):
        pl.when(jnp.logical_and(y == 0, before))(lambda: y_down(s).start())
        pl.when(jnp.logical_and(y == ny - 1, after))(lambda: y_up(s).start())

    def receive_z(s, i):
        pl.when(below)(lambda: z_up(s, i).wait_recv())
        pl.when(above)(lambda: z_down(s, i).wait_recv())

    def receive_y(s, y):
        pl.when(jnp.logical_and(y == 0, before))(lambda: y_up(s).wait_recv())
        pl.when(jnp.logical_and(y == ny - 1, after))(lambda: y_down(s).wait_recv())

    def forward(s, i):
        @pl.when(is_first)
        def _():
            relay_up(s, i).wait_recv()
            forward_up(s, i).start()

        @pl.when(is_last)
        def _():
            relay_down(s, i).wait_recv()
            forward_down(s, i).start()

    small = [
        pltpu.make_async_copy(dirs_hbm, dirs, small_sem.at[0]),
        pltpu.make_async_copy(signs_hbm, signs, small_sem.at[1]),
    ]
    for copy in small:
        copy.start()
    for i in range(ny):
        for z in range(nz):
            load(i * nz + z).start()

    barrier = pltpu.get_barrier_semaphore()
    inner, outer = jnp.logical_or(is_low, is_high), jnp.logical_or(is_first, is_last)
    greeted = [(below, (gz - 1, gy)), (above, (gz + 1, gy)), (before, (gz, gy - 1)), (after, (gz, gy + 1))]
    greeted += [(inner, (0, gy)), (inner, (gz_last, gy)), (outer, (seam_low, gy)), (outer, (seam_high, gy))]
    for there, target in greeted:
        @pl.when(there)
        def _():
            pl.semaphore_signal(barrier, inc=1, device_id=target, device_id_type=MESH)

    @pl.when(gz == 0)
    def _():
        p[0:ITERS, 0] = jnp.zeros_like(p[0:ITERS, 0])

    @pl.when(gz == gz_last)
    def _():
        q[0:ITERS, nz] = jnp.zeros_like(q[0:ITERS, nz])

    @pl.when(gy == 0)
    def _():
        u[:, :, 0] = jnp.zeros_like(u[:, :, 0])

    @pl.when(gy == gy_last)
    def _():
        v[:, :, ny] = jnp.zeros_like(v[:, :, ny])

    for copy in small:
        copy.wait()
    half_speed = TIME_STEP * jnp.abs(dirs[:, 0:LANES])
    sign = signs[:, 0:LANES].astype(jnp.float32)
    sign_z = sign[2:3]
    rows = [half_speed[0:1], half_speed[1:2], half_speed[2:3]]
    rows.append(1.0 - (rows[0] + rows[1] + rows[2]))
    rows += [sign[0:1] * sign_z, sign[1:2] * sign_z, sign_z]
    table = jnp.concatenate(rows + [jnp.zeros((LANES - len(rows), LANES), jnp.float32)], 0).T

    def spread(c):
        coef[c] = jnp.broadcast_to(table[0:HALF, c : c + 1], (HALF, LANES))

    spread(SZ)
    spread(SY)

    peers = sum(there.astype(jnp.int32) for there, _ in greeted)
    pl.semaphore_wait(barrier, peers)

    def first(i, carry):
        y = i
        for z in range(nz):
            r = y * nz + z
            load(r).wait()
            for c in range(0, HALF, CHUNK):
                lines = slice(c, c + CHUNK)
                one, other = stage[r, c : c + CHUNK, :], stage[r, HALF + c : HALF + c + CHUNK, :]
                upward, along_y = coef[SZ, lines] > 0, coef[SY, lines] > 0
                up, down = jnp.where(upward, one, other), jnp.where(upward, other, one)
                p[0, z + 1, y, lines] = up
                q[0, z, y, lines] = down
                u[0, z, y + 1, lines] = jnp.where(along_y, up, down)
                v[0, z, y, lines] = jnp.where(along_y, down, up)
        pl.when(i % ROWS == ROWS - 1)(lambda: send_z(0, i // ROWS))
        send_y(0, y)
        return carry

    lax.fori_loop(0, ny, first, 0)
    for c in (AX, AY, AZ, CENTER, SX):
        spread(c)

    matrix = angular_matrix(dirs, basis, scaled, left, right)[0:HALF, 0:HALF]
    high = matrix.astype(jnp.bfloat16)
    mat_hi[...] = high
    mat_lo[...] = (matrix - high.astype(jnp.float32)).astype(jnp.bfloat16)

    lane = lax.broadcasted_iota(jnp.int32, (CHUNK, LANES), 1)

    def local(s, y):
        receive_y(s, y)
        total = jnp.concatenate([p[s, z + 1, y] + q[s, z, y] for z in range(nz)], 1)
        total_hi = total.astype(jnp.bfloat16)
        total_lo = (total - total_hi.astype(jnp.float32)).astype(jnp.bfloat16)
        hi, lo = mat_hi[...], mat_lo[...]
        angular[...] = (
            jnp.dot(hi, total_hi, preferred_element_type=jnp.float32)
            + jnp.dot(hi, total_lo, preferred_element_type=jnp.float32)
            + jnp.dot(lo, total_hi, preferred_element_type=jnp.float32)
        )
        for z in range(nz):
            for c in range(0, HALF, CHUNK):
                lines = slice(c, c + CHUNK)
                up, down = p[s, z + 1, y, lines], q[s, z, y, lines]
                along_x, along_y = coef[SX, lines] > 0, coef[SY, lines] > 0
                rising, falling = jnp.where(along_x, up, down), jnp.where(along_x, down, up)
                rising = jnp.where(lane == 0, 0.0, pltpu.roll(rising, 1, 1))
                falling = jnp.where(lane == LANES - 1, 0.0, pltpu.roll(falling, LANES - 1, 1))
                y_low, y_high = u[s, z, y, lines], v[s, z, y + 1, lines]
                ang = angular[lines, z * LANES : (z + 1) * LANES]
                ax, ay, az, center = (coef[i, lines] for i in (AX, AY, AZ, CENTER))
                new_up = (
                    center * up + ang + ax * jnp.where(along_x, rising, falling)
                    + ay * jnp.where(along_y, y_low, y_high)
                )
                new_down = (
                    center * down + ang + ax * jnp.where(along_x, falling, rising)
                    + ay * jnp.where(along_y, y_high, y_low)
                )
                if z > 0:
                    new_up += az * p[s, z, y, lines]
                if z < nz - 1:
                    new_down += az * q[s, z + 1, y, lines]
                p[s + 1, z + 1, y, lines] = new_up
                q[s + 1, z, y, lines] = new_down

    def finish(s, y, last):
        pl.when(y % ROWS == 0)(lambda: receive_z(s, y // ROWS))
        for c in range(0, HALF, CHUNK):
            lines = slice(c, c + CHUNK)
            az = coef[AZ, lines]
            for z in range(nz):
                up, down = p[s + 1, z + 1, y, lines], q[s + 1, z, y, lines]
                if z == 0:
                    up += az * p[s, 0, y, lines]
                if z == nz - 1:
                    down += az * q[s, nz, y, lines]
                if last:
                    r = y * nz + z
                    upward = coef[SZ, lines] > 0
                    one, other = jnp.where(upward, up, down), jnp.where(upward, down, up)
                    out[pl.ds(c * ny * nz + r, CHUNK, stride=ny * nz), :] = one
                    out[pl.ds((HALF + c) * ny * nz + r, CHUNK, stride=ny * nz), :] = other
                else:
                    along_y = coef[SY, lines] > 0
                    if z == 0:
                        p[s + 1, 1, y, lines] = up
                    if z == nz - 1:
                        q[s + 1, nz - 1, y, lines] = down
                    u[s + 1, z, y + 1, lines] = jnp.where(along_y, up, down)
                    v[s + 1, z, y, lines] = jnp.where(along_y, down, up)

    def sent(s, i):
        passed = jnp.logical_and(outer, i < RELAYED)
        pl.when(jnp.logical_or(above, passed))(lambda: z_up(s, i).wait_send())
        pl.when(jnp.logical_or(below, passed))(lambda: z_down(s, i).wait_send())

    def y_sent(s):
        pl.when(after)(lambda: y_up(s).wait_send())
        pl.when(before)(lambda: y_down(s).wait_send())

    for i in range(RELAYED):
        forward(0, i)

    def step(s, carry):
        def ahead(i, carry):
            local(s, i)
            pl.when(i % ROWS == ROWS - 1)(lambda: send_z(s + 1, i // ROWS))
            return carry

        def behind(i, carry):
            finish(s, i, False)
            send_y(s + 1, i)
            return carry

        lax.fori_loop(0, ny, ahead, 0)
        lax.fori_loop(0, ny, behind, 0)
        for i in range(RELAYED):
            forward(s + 1, i)
        return carry

    lax.fori_loop(0, ITERS - 1, step, 0)

    def ahead(i, carry):
        for s in range(ITERS - 1):
            pl.when(i < blocks)(lambda s=s: sent(s, i))
        local(ITERS - 1, i)
        return carry

    def behind(i, carry):
        finish(ITERS - 1, i, True)
        return carry

    lax.fori_loop(0, ny, ahead, 0)
    for s in range(ITERS):
        y_sent(s)
    lax.fori_loop(0, ny, behind, 0)
    for i in range(blocks):
        sent(ITERS - 1, i)


def shards(fodf, directions, signs):
    orientations, ny, nz, _ = fodf.shape
    f32, vmem, dma = jnp.float32, pltpu.VMEM, pltpu.SemaphoreType.DMA
    rows = fodf.reshape(orientations, ny * nz, 1, LANES)
    enhanced = pl.pallas_call(
        kernel,
        out_shape=vmem((orientations * ny * nz, LANES), f32),
        in_specs=[pl.BlockSpec(memory_space=pltpu.HBM)] * 3,
        out_specs=pl.BlockSpec(memory_space=vmem),
        scratch_shapes=[
            vmem((ny * nz, orientations, LANES), f32),
            vmem((3, orientations), f32),
            vmem((3, orientations), jnp.int32),
            vmem((7, HALF, LANES), f32),
            vmem((MODES_PAD, LANES), f32),
            vmem((MODES_PAD, LANES), f32),
            vmem((MODES_PAD, LANES), f32),
            vmem((MODES_PAD, LANES), f32),
            vmem((HALF, HALF), jnp.bfloat16),
            vmem((HALF, HALF), jnp.bfloat16),
            vmem((HALF, nz * LANES), f32),
            vmem((ITERS + 1, nz + 1, ny, HALF, LANES), f32),
            vmem((ITERS + 1, nz + 1, ny, HALF, LANES), f32),
            vmem((ITERS, nz, ny + 1, HALF, LANES), f32),
            vmem((ITERS, nz, ny + 1, HALF, LANES), f32),
            vmem((ITERS, RELAYED, ROWS, HALF, LANES), f32),
            dma((ny * nz,)),
            dma((2,)),
            dma((2, ITERS, ny // ROWS)),
            dma((2, ITERS, ny // ROWS)),
            dma((2, ITERS)),
            dma((2, ITERS)),
            dma((ITERS, RELAYED)),
        ],
        compiler_params=pltpu.CompilerParams(
            collective_id=0, has_side_effects=True, vmem_limit_bytes=48 * 1024 * 1024
        ),
    )(*(pltpu.with_memory_space_constraint(a, pltpu.HBM) for a in (rows, directions, signs)))
    return enhanced.reshape(fodf.shape)


def solution(mesh):
    placed = (P(None, "gy", "gz", None), P(), P())
    return jax.shard_map(
        shards, mesh=mesh, in_specs=placed, out_specs=P(None, "gy", "gz", None), check_vma=False
    )
```
